512 devices in a mesh: ctx: 16 (over z, core), exp: 32 (over y, x).
Axes of the slice: x: 4, y: 8, z: 8, core: 2. Of those that a mesh axis runs over, the one named last changes fastest.
Arguments:
- tokens: bfloat16 [65536, 2048], P(('ctx', 'exp')), may hold values from -6 to 6
- cotangent: bfloat16 [65536, 2048], P(('ctx', 'exp')), may hold values from -6 to 6
- expert_ids: int32 [2, 65536, 1], P(None, ('ctx', 'exp')), may hold values from 0 to 31
- weight_in: bfloat16 [32, 2048, 256], P('exp', 'ctx'), may hold values from -0.125 to 0.125
- weight_out: bfloat16 [32, 256, 2048], P('exp', None, 'ctx'), may hold values from -0.375 to 0.375
- router: bfloat16 [2048, 32], P('ctx', 'exp'), may hold values from -0.125 to 0.125
Outputs:
- grad_in: float32 [32, 2048, 256], P('exp', 'ctx')
- grad_out: float32 [32, 256, 2048], P('exp', None, 'ctx')
The draws below stay inside these ranges and needn't reach their ends.
Inputs may be any that keep to these rules, and one draw needn't show every extreme that they name: `expert_ids`: each token chooses one expert in each recurrence; every expert is chosen by some token.
All inputs are finite; a program needn't handle non-finite values.
Results may differ from the reference program's by a relative error of at most 0.023.
Values may be sent and summed in bfloat16 or wider, within the bound.
No kernel may reach another device: no remote copies, remote signals or barrier semaphores. Data moves between devices by JAX's collectives and lax.ppermute only.
A program may use at most 64 MiB of HBM per device.

```python
import jax
import jax.numpy as jnp
from jax import lax

D = 2048
G = 256
TOK_DEV = 128
EXPERTS = 32
CAP = 3
TOKENS = 65536
N_CTX = 16


def block_scale(key, extent, cuts, smallest, top_value):
    loudness = 1.0
    for axis_at, blocks in cuts:
        steps = jax.random.uniform(jax.random.fold_in(jax.random.fold_in(key, 6), axis_at), (blocks,), jnp.float32, smallest / len(cuts), top_value / len(cuts))
        loudness = loudness * jnp.repeat(jnp.exp(steps), extent[axis_at] // blocks).reshape((-1,) + (1,) * (len(extent) - 1 - axis_at))
    return loudness


def distinct(key, rows, amount, top, lift):
    ranking = jax.random.permutation(jax.random.fold_in(key, 1), amount)
    favour = ranking
    for power in range(3):
        favour = favour * favour // amount
    favour = favour * lift // amount
    lots = jax.random.randint(jax.random.fold_in(key, 2), (rows, amount), 0, 4096) + favour
    sure = jax.random.permutation(jax.random.fold_in(key, 3), rows)[jnp.arange(amount) % rows]
    lots = jnp.where(jnp.arange(rows)[:, None] == sure[None, :], 1 << 14, lots)
    priority = lots * amount + jnp.arange(amount)
    return lax.top_k(priority.astype(jnp.int32), top)[1].astype(jnp.int32)


def noise(rng, extent, spread, limit, pieces=(), kind=jnp.bfloat16):
    entries = spread * jax.random.normal(rng, extent, jnp.float32)
    if pieces:
        entries = entries * block_scale(rng, extent, pieces, -0.22, 0.18)
    return jnp.clip(entries, -limit, limit).astype(kind)


def setup_inputs(seed: int = 0) -> dict:
    key_of = jax.random.split(jax.random.key(seed), 7)
    return {
        "tokens": noise(key_of[0], (TOKENS, D), 1.0, 6.0, ((0, 512),)),
        "cotangent": noise(key_of[1], (TOKENS, D), 1.0, 6.0, ((0, 512),)),
        "expert_ids": distinct(key_of[2], 2 * TOKENS, EXPERTS, 1, 256).reshape((2, TOKENS, 1)),
        "weight_in": noise(key_of[3], (EXPERTS, D, G), D ** -0.5, 0.125, ((0, 32), (1, 16))),
        "weight_out": noise(key_of[4], (EXPERTS, G, D), G ** -0.5, 0.375, ((0, 32), (2, 16))),
        "router": noise(key_of[5], (D, EXPERTS), D ** -0.5, 0.125, ((0, 16), (1, 32))),
    }


epsilon = 1e-06

def normalize(state):
    scale_row = jnp.sqrt(lax.optimization_barrier(jnp.mean(state * state, axis=-1, keepdims=True)) + epsilon)
    return (state / scale_row, scale_row)

def norm_backward(upstream, unit, scale_row):
    return (upstream - unit * lax.optimization_barrier(jnp.mean(upstream * unit, axis=-1, keepdims=True))) / scale_row

def route_table(chosen):
    sources = TOKENS // TOK_DEV
    onehot = (chosen[:, None] == jnp.arange(EXPERTS, dtype=jnp.int32)[None, :]).astype(jnp.int32)
    blocked = onehot.reshape(sources, TOK_DEV, EXPERTS)
    before = (jnp.cumsum(blocked, axis=1).astype(jnp.int32) - blocked).reshape(TOKENS, EXPERTS)
    position = lax.optimization_barrier(jnp.sum(before * onehot, axis=1)).astype(jnp.int32)
    kept = position < CAP
    anchor = jnp.arange(TOKENS, dtype=jnp.int32) // TOK_DEV
    target = jnp.where(kept, chosen, EXPERTS).astype(jnp.int32)
    place = (anchor * CAP + jnp.minimum(position, CAP - 1)).astype(jnp.int32)
    table = jnp.full((EXPERTS, sources * CAP), TOKENS, dtype=jnp.int32)
    return table.at[target, place].set(jnp.arange(TOKENS, dtype=jnp.int32), mode='drop')

def take_rows(values, table):
    padded = jnp.concatenate([values, jnp.zeros((1, values.shape[1]), values.dtype)], axis=0)
    return padded[table]

def put_rows(stacked, table):
    flat = stacked.reshape(-1, stacked.shape[-1])
    target = jnp.zeros((TOKENS + 1, stacked.shape[-1]), stacked.dtype)
    return target.at[table.reshape(-1)].set(flat)[:TOKENS]

def expert_forward(rows, weight_a, weight_b, column):
    before_relu = jnp.dot(rows, weight_a, preferred_element_type=jnp.float32)
    positive = jnp.maximum(before_relu, 0.0)
    hidden = (positive * positive).astype(jnp.bfloat16)
    expert_out = jnp.dot(hidden, weight_b, preferred_element_type=jnp.float32)
    logit = jnp.dot(rows, column, preferred_element_type=jnp.float32)
    gate_value = jax.nn.sigmoid(logit)
    return (before_relu, hidden, expert_out, gate_value)

def expert_backward(upstream, weight_b, parts):
    before_relu, hidden, expert_out, gate_value = parts
    upper = upstream.astype(jnp.float32)
    grad_expert = (gate_value * upper).astype(jnp.bfloat16)
    grad_gate = lax.optimization_barrier(jnp.sum(upper * expert_out, axis=1, keepdims=True))
    grad_logit = grad_gate * gate_value * (1.0 - gate_value)
    grad_hidden = lax.dot_general(grad_expert, weight_b, (((1,), (1,)), ((), ())), preferred_element_type=jnp.float32)
    grad_pre = (grad_hidden * 2.0 * jnp.maximum(before_relu, 0.0)).astype(jnp.bfloat16)
    return (grad_expert, grad_pre, grad_logit)

def row_gradient(grad_pre, grad_logit, weight_a, column):
    flowing = lax.dot_general(grad_pre, weight_a, (((1,), (1,)), ((), ())), preferred_element_type=jnp.float32)
    return (flowing + grad_logit * column[:, 0].astype(jnp.float32)[None, :]).astype(jnp.bfloat16)

def group_product(left, right):
    left_g = left.reshape(N_CTX, -1, left.shape[1]).astype(jnp.float32)
    right_g = right.reshape(N_CTX, -1, right.shape[1]).astype(jnp.float32)
    return jnp.einsum('crd,crg->cdg', left_g, right_g)

def round_sum(partial_value):
    rounded = lax.optimization_barrier(partial_value.astype(jnp.bfloat16))
    return lax.optimization_barrier(jnp.sum(rounded.astype(jnp.float32), axis=0))

def reference(tokens, cotangent, expert_ids, weight_in, weight_out, router):
    first = route_table(expert_ids[0, :, 0])
    second = route_table(expert_ids[1, :, 0])
    columns = router.T
    state_zero = tokens.astype(jnp.float32)
    unit_zero, scale_zero = normalize(state_zero)
    routed_zero = unit_zero.astype(jnp.bfloat16)

    def forward_expert(item):
        table, weight_a, weight_b, column = item
        parts = expert_forward(take_rows(routed_zero, table), weight_a, weight_b, column[:, None])
        return (parts[3] * parts[2]).astype(jnp.bfloat16)
    mixed = lax.map(forward_expert, (first, weight_in, weight_out, columns))
    state_one = state_zero + put_rows(mixed, first).astype(jnp.float32)
    unit_one, scale_one = normalize(state_one)
    routed_one = unit_one.astype(jnp.bfloat16)

    def second_expert(item):
        table, weight_a, weight_b, column = item
        rows = take_rows(routed_one, table)
        parts = expert_forward(rows, weight_a, weight_b, column[:, None])
        grad_expert, grad_pre, grad_logit = expert_backward(take_rows(cotangent, table), weight_b, parts)
        return row_gradient(grad_pre, grad_logit, weight_a, column[:, None])
    returned = lax.map(second_expert, (second, weight_in, weight_out, columns))
    grad_unit = put_rows(returned, second).astype(jnp.float32)
    grad_state = cotangent.astype(jnp.float32) + norm_backward(grad_unit, unit_one, scale_one)
    upstream_zero = grad_state.astype(jnp.bfloat16)

    def weight_grads(item):
        table_a, table_b, weight_a, weight_b, column = item
        rows_b = take_rows(routed_one, table_b)
        parts_b = expert_forward(rows_b, weight_a, weight_b, column[:, None])
        gout_b, gpre_b, unused_b = expert_backward(take_rows(cotangent, table_b), weight_b, parts_b)
        rows_a = take_rows(routed_zero, table_a)
        parts_a = expert_forward(rows_a, weight_a, weight_b, column[:, None])
        gout_a, gpre_a, unused_a = expert_backward(take_rows(upstream_zero, table_a), weight_b, parts_a)
        part_in = group_product(rows_a, gpre_a) + group_product(rows_b, gpre_b)
        part_out = group_product(parts_a[1], gout_a) + group_product(parts_b[1], gout_b)
        return (round_sum(part_in), round_sum(part_out))
    grad_in, grad_out = lax.map(weight_grads, (first, second, weight_in, weight_out, columns))
    return (grad_in, grad_out)
```

```python
import functools

import jax
import jax.numpy as jnp
from jax import lax
from jax.experimental import pallas as pl
from jax.experimental.pallas import tpu as pltpu
from jax.sharding import PartitionSpec as P

epsilon = 1e-06
TOK, D, G, EXPERTS, CAP = 128, 2048, 256, 32, 3
SLOTS = EXPERTS * CAP
LANE = 128
CHUNKS = D // LANE
PEER = CAP * CHUNKS
CHIPS = 8
SHARD = 2 * G + 16
bf16, f32 = jnp.bfloat16, jnp.float32


def iota(shape, dimension):
    return lax.broadcasted_iota(jnp.int32, shape, dimension)


def choose(ids):
    hit = iota((EXPERTS, TOK), 0) == ids
    earlier = jnp.where(iota((TOK, TOK), 0) < iota((TOK, TOK), 1), 1.0, 0.0).astype(bf16)
    before = jnp.dot(jnp.where(hit, 1.0, 0.0).astype(bf16), earlier, preferred_element_type=f32)
    position = jnp.sum(jnp.where(hit, before, 0.0), axis=0, keepdims=True).astype(jnp.int32)
    slot = jnp.where(position < CAP, position * EXPERTS + ids, -1)
    return jnp.where(iota((SLOTS, TOK), 0) == slot, 1.0, 0.0).astype(bf16)


def to_slots(pick, rows):
    return jnp.dot(pick, rows, preferred_element_type=f32)


def to_tokens(pick, rows):
    return lax.dot_general(pick, rows, (((0,), (0,)), ((), ())), preferred_element_type=f32)


def pack(rows, wide, stride=PEER, first=0):
    for r in range(CAP):
        for k in range(CHUNKS):
            wide[pl.ds(first + r * CHUNKS + k, EXPERTS, stride=stride), :] = rows[
                r * EXPERTS : (r + 1) * EXPERTS, k * LANE : (k + 1) * LANE
            ]


def unpack(wide, dense, stride=PEER, first=0):
    for r in range(CAP):
        for k in range(CHUNKS):
            dense[r * EXPERTS : (r + 1) * EXPERTS, k * LANE : (k + 1) * LANE] = wide[
                pl.ds(first + r * CHUNKS + k, EXPERTS, stride=stride), :
            ].astype(dense.dtype)


def normalize(state):
    scale = jnp.sqrt(jnp.mean(state * state, axis=-1, keepdims=True) + epsilon)
    return state / scale, scale


def weights_of(gathered, wa, wb, column):
    for c in range(2 * CHIPS):
        at, to = c * SHARD, c * LANE
        wa[to : to + LANE, :LANE] = gathered[at : at + LANE, :]
        wa[to : to + LANE, LANE:] = gathered[at + LANE : at + 2 * LANE, :]
        wb[:, to : to + LANE] = gathered[at + G : at + 2 * G, :]
        column[:, to : to + LANE] = gathered[at + 2 * G : at + 2 * G + 1, :].astype(f32)


def forward(rows, wa, wb, column):
    before = jnp.dot(rows, wa[...], preferred_element_type=f32)
    positive = jnp.maximum(before, 0.0)
    hidden = (positive * positive).astype(bf16)
    expert_out = jnp.dot(hidden, wb[...], preferred_element_type=f32)
    logit = jnp.sum(rows.astype(f32) * column[...], axis=1, keepdims=True)
    gate = 1.0 / (1.0 + jnp.exp(-logit))
    return positive, hidden, expert_out, gate


def backward(upstream, wb, positive, gate):
    upper = upstream.astype(f32)
    grad_expert = (gate * upper).astype(bf16)
    grad_hidden = lax.dot_general(
        grad_expert, wb[...], (((1,), (1,)), ((), ())), preferred_element_type=f32
    )
    grad_pre = (grad_hidden * 2.0 * positive).astype(bf16)
    return upper, grad_expert, grad_pre


def dispatch_kernel(tokens, cotangent, ids, out, wide):
    unit, _ = normalize(tokens[...].astype(f32))
    pack(to_slots(choose(ids[0:1, :]), unit.astype(bf16)), wide, 2 * PEER, 0)
    pack(to_slots(choose(ids[1:2, :]), cotangent[...]), wide, 2 * PEER, PEER)
    out[...] = wide[...].astype(bf16)


def arrive_kernel(taken, rows, upstream, wide):
    wide[...] = taken[...].astype(f32)
    unpack(wide, rows, 2 * PEER, 0)
    unpack(wide, upstream, 2 * PEER, PEER)


def first_kernel(rows, gathered, out, positive_out, hidden_out, gate_out, wa, wb, column, wide):
    weights_of(gathered, wa, wb, column)
    positive, hidden, expert_out, gate = forward(rows[...], wa, wb, column)
    pack((gate * expert_out), wide)
    out[...] = wide[...].astype(bf16)
    positive_out[...] = positive
    hidden_out[...] = hidden
    gate_out[...] = jnp.broadcast_to(gate, (SLOTS, LANE))


def middle_kernel(tokens, ids, mixed, out, state_out, wide, dense):
    wide[...] = mixed[...].astype(f32)
    unpack(wide, dense)
    state = tokens[...].astype(f32) + to_tokens(choose(ids[0:1, :]), dense[...])
    state_out[...] = state
    unit, _ = normalize(state)
    pack(to_slots(choose(ids[1:2, :]), unit.astype(bf16)), wide)
    out[...] = wide[...].astype(bf16)


def second_kernel(
    taken, upstream, gathered, out, rows, expert_grad, pre_grad, hidden_out, wa, wb, column, wide
):
    wide[...] = taken[...].astype(f32)
    unpack(wide, rows)
    weights_of(gathered, wa, wb, column)
    positive, hidden, expert_out, gate = forward(rows[...], wa, wb, column)
    upper, grad_expert, grad_pre = backward(upstream[...], wb, positive, gate)
    grad_gate = jnp.sum(upper * expert_out, axis=1, keepdims=True)
    grad_logit = grad_gate * gate * (1.0 - gate)
    flowing = lax.dot_general(
        grad_pre, wa[...], (((1,), (1,)), ((), ())), preferred_element_type=f32
    )
    pack(flowing + grad_logit * column[...], wide)
    out[...] = wide[...].astype(bf16)
    expert_grad[...] = grad_expert
    pre_grad[...] = grad_pre
    hidden_out[...] = hidden


def return_kernel(cotangent, state, ids, taken, out, wide, dense):
    wide[...] = taken[...].astype(f32)
    unpack(wide, dense)
    unit, scale = normalize(state[...])
    grad = to_tokens(choose(ids[1:2, :]), dense[...])
    inner = jnp.mean(grad * unit, axis=-1, keepdims=True)
    upstream = cotangent[...].astype(f32) + (grad - unit * inner) / scale
    pack(to_slots(choose(ids[0:1, :]), upstream.astype(bf16)), wide)
    out[...] = wide[...].astype(bf16)


def weight_kernel(
    taken, gathered, rows_zero, positive, hidden_zero, gate,
    rows_one, expert_one, pre_one, hidden_one,
    mine, other, wide, dense, wb, part
):
    wide[...] = taken[...].astype(f32)
    unpack(wide, dense)
    for c in range(2 * CHIPS):
        wb[:, c * LANE : (c + 1) * LANE] = gathered[c * SHARD + G : c * SHARD + 2 * G, :]
    _, grad_expert, grad_pre = backward(dense[...], wb, positive[...], gate[:, :1])
    over_rows = (((0,), (0,)), ((), ()))
    part[:G, :] = lax.dot_general(
        grad_pre, rows_zero[...], over_rows, preferred_element_type=f32
    ) + lax.dot_general(pre_one[...], rows_one[...], over_rows, preferred_element_type=f32)
    part[G:, :] = lax.dot_general(
        hidden_zero[...], grad_expert, over_rows, preferred_element_type=f32
    ) + lax.dot_general(hidden_one[...], expert_one[...], over_rows, preferred_element_type=f32)
    core = lax.rem(lax.axis_index("ctx"), 2)
    for z in range(CHIPS):
        here = pl.multiple_of((2 * z + core) * LANE, LANE)
        there = pl.multiple_of((2 * z + 1 - core) * LANE, LANE)
        mine[z] = part[:, pl.ds(here, LANE)].astype(bf16)
        other[z] = part[:, pl.ds(there, LANE)].astype(bf16)


def pair_kernel(mine, other, out):
    out[...] = (mine[...].astype(f32) + other[...].astype(f32)).astype(bf16)


def total_kernel(parts, grad_in, grad_out):
    total = parts[0].astype(f32)
    for z in range(1, CHIPS):
        total = total + parts[z].astype(f32)
    grad_in[0] = total[:G, :].T
    grad_out[0] = total[G:, :]


def call(kernel, outs, scratch=(), **params):
    return pl.pallas_call(
        kernel,
        out_shape=[jax.ShapeDtypeStruct(s, t) for s, t in outs],
        scratch_shapes=[pltpu.VMEM(s, t) for s, t in scratch],
        compiler_params=pltpu.CompilerParams(vmem_limit_bytes=24 << 20, **params),
    )


PACKED = ((EXPERTS * PEER, LANE), bf16)
WIDE = ((EXPERTS * PEER, LANE), f32)
DENSE = ((SLOTS, D), bf16)
NARROW = ((SLOTS, G), bf16)
WEIGHTS = (((D, G), bf16), ((G, D), bf16), ((1, D), f32))


def over_exp(buffer):
    shaped = buffer.reshape(EXPERTS, -1, LANE)
    return lax.all_to_all(shaped, "exp", 0, 0, tiled=True).reshape(buffer.shape)


def on_device(tokens, cotangent, expert_ids, weight_in, weight_out, router):
    chips = lax.axis_size("ctx") // 2
    ids = expert_ids[:, :, 0]
    shard = jnp.concatenate(
        [
            weight_in[0, :, :LANE],
            weight_in[0, :, LANE:],
            weight_out[0],
            jnp.pad(router.reshape(1, LANE), ((0, 15), (0, 0))),
        ],
        axis=0,
    )
    gathered = lax.all_gather(shard, "ctx", axis=0, tiled=True)
    wide_two = ((2 * EXPERTS * PEER, LANE), f32)
    (leaving,) = call(dispatch_kernel, [((2 * EXPERTS * PEER, LANE), bf16)], [wide_two])(
        tokens, cotangent, ids
    )
    rows_zero, upstream_one = call(arrive_kernel, [DENSE, DENSE], [wide_two])(over_exp(leaving))
    mixed, positive, hidden_zero, gate = call(
        first_kernel,
        [PACKED, ((SLOTS, G), f32), NARROW, ((SLOTS, LANE), f32)],
        [*WEIGHTS, WIDE],
    )(rows_zero, gathered)
    leaving, state_one = call(middle_kernel, [PACKED, ((TOK, D), f32)], [WIDE, DENSE])(
        tokens, ids, over_exp(mixed)
    )
    leaving, rows_one, expert_one, pre_one, hidden_one = call(
        second_kernel, [PACKED, DENSE, DENSE, NARROW, NARROW], [*WEIGHTS, WIDE]
    )(over_exp(leaving), upstream_one, gathered)
    (leaving,) = call(return_kernel, [PACKED], [WIDE, DENSE])(
        cotangent, state_one, ids, over_exp(leaving)
    )
    block = ((CHIPS, 2 * G, LANE), bf16)
    mine, other = call(
        weight_kernel, [block, block], [WIDE, DENSE, WEIGHTS[1], ((2 * G, D), f32)]
    )(
        over_exp(leaving), gathered, rows_zero, positive, hidden_zero, gate,
        rows_one, expert_one, pre_one, hidden_one,
    )
    across = [(2 * z + c, 2 * z + 1 - c) for z in range(chips) for c in range(2)]
    (pair,) = call(pair_kernel, [block])(mine, lax.ppermute(other, "ctx", across))
    columns = [[2 * z + c for z in range(chips)] for c in range(2)]
    parts = lax.all_to_all(pair, "ctx", 0, 0, tiled=True, axis_index_groups=columns)
    grad_in, grad_out = call(total_kernel, [((1, LANE, G), f32), ((1, G, LANE), f32)])(parts)
    return (grad_in, grad_out)


def solution(mesh):
    placed = (
        P(("ctx", "exp"), None),
        P(("ctx", "exp"), None),
        P(None, ("ctx", "exp"), None),
        P("exp", "ctx", None),
        P("exp", None, "ctx"),
        P("ctx", "exp"),
    )
    return jax.shard_map(
        on_device,
        mesh=mesh,
        in_specs=placed,
        out_specs=(P("exp", "ctx", None), P("exp", None, "ctx")),
        check_vma=False,
    )
```

```python
import functools

import jax
import jax.numpy as jnp
from jax import lax
from jax.experimental import pallas as pl
from jax.experimental.pallas import tpu as pltpu
from jax.sharding import PartitionSpec as P

epsilon = 1e-06
TOK, D, G, EXPERTS, CAP = 128, 2048, 256, 32, 3
SLOTS = EXPERTS * CAP
LANE = 128
CHUNKS = D // LANE
PEER = CAP * CHUNKS
CHIPS = 8
SHARD = 2 * G + 16
bf16, f32 = jnp.bfloat16, jnp.float32


def iota(shape, dimension):
    return lax.broadcasted_iota(jnp.int32, shape, dimension)


def choose(ids):
    hit = iota((EXPERTS, TOK), 0) == ids
    earlier = jnp.where(iota((TOK, TOK), 0) < iota((TOK, TOK), 1), 1.0, 0.0).astype(bf16)
    before = jnp.dot(jnp.where(hit, 1.0, 0.0).astype(bf16), earlier, preferred_element_type=f32)
    position = jnp.sum(jnp.where(hit, before, 0.0), axis=0, keepdims=True).astype(jnp.int32)
    slot = jnp.where(position < CAP, position * EXPERTS + ids, -1)
    return jnp.where(iota((SLOTS, TOK), 0) == slot, 1.0, 0.0).astype(bf16)


def to_slots(pick, rows):
    return jnp.dot(pick, rows, preferred_element_type=f32)


def to_tokens(pick, rows):
    return lax.dot_general(pick, rows, (((0,), (0,)), ((), ())), preferred_element_type=f32)


def pack(rows, wide, stride=PEER, first=0):
    for r in range(CAP):
        for k in range(CHUNKS):
            wide[pl.ds(first + r * CHUNKS + k, EXPERTS, stride=stride), :] = rows[
                r * EXPERTS : (r + 1) * EXPERTS, k * LANE : (k + 1) * LANE
            ]


def unpack(wide, dense, stride=PEER, first=0):
    for r in range(CAP):
        for k in range(CHUNKS):
            dense[r * EXPERTS : (r + 1) * EXPERTS, k * LANE : (k + 1) * LANE] = wide[
                pl.ds(first + r * CHUNKS + k, EXPERTS, stride=stride), :
            ].astype(dense.dtype)


def normalize(state):
    scale = jnp.sqrt(jnp.mean(state * state, axis=-1, keepdims=True) + epsilon)
    return state / scale, scale


def share_kernel(weight_in, weight_out, router, out):
    out[:LANE, :] = weight_in[0, :, :LANE]
    out[LANE:G, :] = weight_in[0, :, LANE:]
    out[G : 2 * G, :] = weight_out[0]
    out[2 * G :, :] = jnp.broadcast_to(router[...], (SHARD - 2 * G, LANE))


def place(block, first, chip, wa, wb, column):
    for core in range(2):
        at = first + core * SHARD
        to = pl.ds(pl.multiple_of((2 * chip + core) * LANE, LANE), LANE)
        wa[to, :LANE] = block[at : at + LANE, :]
        wa[to, LANE:] = block[at + LANE : at + G, :]
        wb[:, to] = block[at + G : at + 2 * G, :]
        column[:, to] = block[at + 2 * G : at + 2 * G + 1, :].astype(f32)


def forward(rows, wa, wb, column):
    before = jnp.dot(rows, wa[...], preferred_element_type=f32)
    positive = jnp.maximum(before, 0.0)
    hidden = (positive * positive).astype(bf16)
    expert_out = jnp.dot(hidden, wb[...], preferred_element_type=f32)
    logit = jnp.sum(rows.astype(f32) * column[...], axis=1, keepdims=True)
    gate = 1.0 / (1.0 + jnp.exp(-logit))
    return positive, hidden, expert_out, gate


def backward(upstream, wb, positive, gate):
    upper = upstream.astype(f32)
    grad_expert = (gate * upper).astype(bf16)
    grad_hidden = lax.dot_general(
        grad_expert, wb[...], (((1,), (1,)), ((), ())), preferred_element_type=f32
    )
    grad_pre = (grad_hidden * 2.0 * positive).astype(bf16)
    return upper, grad_expert, grad_pre


def dispatch_kernel(tokens, cotangent, ids, out, wide):
    unit, _ = normalize(tokens[...].astype(f32))
    pack(to_slots(choose(ids[0:1, :]), unit.astype(bf16)), wide, 2 * PEER, 0)
    pack(to_slots(choose(ids[1:2, :]), cotangent[...]), wide, 2 * PEER, PEER)
    out[...] = wide[...].astype(bf16)


def arrive_kernel(taken, rows, upstream, wide):
    wide[...] = taken[...].astype(f32)
    unpack(wide, rows, 2 * PEER, 0)
    unpack(wide, upstream, 2 * PEER, PEER)


def first_kernel(
    rows, own, pair_1, pair_2, pair_3, far,
    out, positive_out, kept, gate_out, wa, wb, column, wide
):
    chip = lax.div(lax.axis_index("ctx"), 2)
    place(own, 0, chip, wa, wb, column)
    for hop, pair in enumerate((pair_1, pair_2, pair_3), 1):
        place(pair, 0, lax.rem(chip + CHIPS - hop, CHIPS), wa, wb, column)
        place(pair, 2 * SHARD, lax.rem(chip + hop, CHIPS), wa, wb, column)
    place(far, 0, lax.rem(chip + CHIPS // 2, CHIPS), wa, wb, column)
    positive, hidden, expert_out, gate = forward(rows[...], wa, wb, column)
    pack((gate * expert_out), wide)
    out[...] = wide[...].astype(bf16)
    positive_out[...] = positive
    kept[:, :D] = rows[...]
    kept[:, D:] = hidden
    gate_out[...] = jnp.broadcast_to(gate, (SLOTS, LANE))


def middle_kernel(tokens, ids, mixed, out, state_out, wide, dense):
    wide[...] = mixed[...].astype(f32)
    unpack(wide, dense)
    state = tokens[...].astype(f32) + to_tokens(choose(ids[0:1, :]), dense[...])
    state_out[...] = state
    unit, _ = normalize(state)
    pack(to_slots(choose(ids[1:2, :]), unit.astype(bf16)), wide)
    out[...] = wide[...].astype(bf16)


def second_kernel(
    taken, upstream, wa, wb, column, out, kept, grads, wide, dense
):
    wide[...] = taken[...].astype(f32)
    unpack(wide, dense)
    positive, hidden, expert_out, gate = forward(dense[...], wa, wb, column)
    upper, grad_expert, grad_pre = backward(upstream[...], wb, positive, gate)
    grad_gate = jnp.sum(upper * expert_out, axis=1, keepdims=True)
    grad_logit = grad_gate * gate * (1.0 - gate)
    flowing = lax.dot_general(
        grad_pre, wa[...], (((1,), (1,)), ((), ())), preferred_element_type=f32
    )
    pack(flowing + grad_logit * column[...], wide)
    out[...] = wide[...].astype(bf16)
    kept[:, :D] = dense[...]
    kept[:, D:] = hidden
    grads[:, :D] = grad_expert
    grads[:, D:] = grad_pre


def return_kernel(cotangent, state, ids, taken, out, wide, dense):
    wide[...] = taken[...].astype(f32)
    unpack(wide, dense)
    unit, scale = normalize(state[...])
    grad = to_tokens(choose(ids[1:2, :]), dense[...])
    inner = jnp.mean(grad * unit, axis=-1, keepdims=True)
    upstream = cotangent[...].astype(f32) + (grad - unit * inner) / scale
    pack(to_slots(choose(ids[0:1, :]), upstream.astype(bf16)), wide)
    out[...] = wide[...].astype(bf16)


def over_rows(left, right):
    return lax.dot_general(left, right, (((0,), (0,)), ((), ())), preferred_element_type=f32)


def first_grad_kernel(taken, wb, positive, gate, out, wide, dense):
    wide[...] = taken[...].astype(f32)
    unpack(wide, dense)
    _, grad_expert, grad_pre = backward(dense[...], wb, positive[...], gate[:, :1])
    out[:, :D] = grad_expert
    out[:, D:] = grad_pre


def weight_kernel(grads_zero, kept_zero, grads_one, kept_one, out, rows, grads, parts):
    core = lax.rem(lax.axis_index("ctx"), 2)
    parts_in = ((grads_zero, kept_zero), (grads_one, kept_one))
    for at, (grad, kept) in zip((0, 2 * SLOTS), parts_in):
        to = slice(at, at + 2 * SLOTS)
        for z in range(CHIPS):
            own = pl.ds(pl.multiple_of((2 * z + core) * LANE, LANE), LANE)
            rows[to, z * LANE : (z + 1) * LANE] = kept[:, own]
            grads[to, z * LANE : (z + 1) * LANE] = grad[:, own]
        parts[to, :G] = grad[:, D:]
        parts[to, G:] = kept[:, D:]
    part_in = over_rows(parts[:, :G], rows[...])
    part_out = over_rows(parts[:, G:], grads[...])
    for z in range(CHIPS):
        at = slice(z * LANE, (z + 1) * LANE)
        out[z, :G, :] = part_in[:, at].astype(bf16)
        out[z, G:, :] = part_out[:, at].astype(bf16)


def total_kernel(parts, grad_in, grad_out):
    total = parts[0].astype(f32)
    for z in range(1, CHIPS):
        total = total + parts[z].astype(f32)
    grad_in[0] = total[:G, :].T
    grad_out[0] = total[G:, :]


def call(kernel, outs, scratch=(), room=24):
    return pl.pallas_call(
        kernel,
        out_shape=[jax.ShapeDtypeStruct(s, t) for s, t in outs],
        scratch_shapes=[pltpu.VMEM(s, t) for s, t in scratch],
        compiler_params=pltpu.CompilerParams(vmem_limit_bytes=room << 20),
    )


PACKED = ((EXPERTS * PEER, LANE), bf16)
WIDE = ((EXPERTS * PEER, LANE), f32)
DENSE = ((SLOTS, D), bf16)
KEPT = ((SLOTS, D + G), bf16)
WEIGHTS = (((D, G), bf16), ((G, D), bf16), ((1, D), f32))


def over_exp(buffer):
    shaped = buffer.reshape(EXPERTS, -1, LANE)
    return lax.all_to_all(shaped, "exp", 0, 0, tiled=True).reshape(buffer.shape)


def on_device(tokens, cotangent, expert_ids, weight_in, weight_out, router):
    chips = lax.axis_size("ctx") // 2
    ids = expert_ids[:, :, 0]
    cores = [[2 * z, 2 * z + 1] for z in range(chips)]

    def both_cores(value):
        return lax.all_gather(value, "ctx", axis=0, tiled=True, axis_index_groups=cores)

    around = [(2 * z, 2 * ((z + 1) % chips)) for z in range(chips)]
    around += [(2 * z + 1, 2 * ((z - 1) % chips) + 1) for z in range(chips)]
    (share,) = call(share_kernel, [((SHARD, LANE), bf16)], room=60)(
        weight_in, weight_out, router.reshape(1, LANE)
    )
    own = both_cores(share)
    passing, pairs = own, []
    for hop in range(chips // 2):
        if hop > 1:
            passing, pairs[hop - 2] = lax.optimization_barrier((passing, both_cores(pairs[hop - 2])))
        passing = lax.ppermute(passing, "ctx", around)
        pairs.append(passing)
        if hop == 0:
            first_hop = passing
    pairs[2] = both_cores(pairs[2])
    wide_two = ((2 * EXPERTS * PEER, LANE), f32)
    (leaving,) = call(dispatch_kernel, [((2 * EXPERTS * PEER, LANE), bf16)], [wide_two], room=60)(
        tokens, cotangent, ids
    )
    leaving, _ = lax.optimization_barrier((leaving, first_hop))
    rows_zero, upstream_one = call(arrive_kernel, [DENSE, DENSE], [wide_two])(over_exp(leaving))
    mixed, positive, kept_zero, gate, wa, wb, column = call(
        first_kernel,
        [PACKED, ((SLOTS, G), f32), KEPT, ((SLOTS, LANE), f32), *WEIGHTS],
        [WIDE],
    )(rows_zero, own, *pairs)
    leaving, state_one = call(middle_kernel, [PACKED, ((TOK, D), f32)], [WIDE, DENSE])(
        tokens, ids, over_exp(mixed)
    )
    leaving, kept_one, grads_one = call(second_kernel, [PACKED, KEPT, KEPT], [WIDE, DENSE])(
        over_exp(leaving), upstream_one, wa, wb, column
    )
    (leaving,) = call(return_kernel, [PACKED], [WIDE, DENSE])(
        cotangent, state_one, ids, over_exp(leaving)
    )
    (grads_zero,) = call(first_grad_kernel, [KEPT], [WIDE, DENSE])(
        over_exp(leaving), wb, positive, gate
    )
    half = ((4 * SLOTS, D // 2), bf16)
    (pair,) = call(
        weight_kernel, [((CHIPS, 2 * G, LANE), bf16)], [half, half, ((4 * SLOTS, 2 * G), bf16)]
    )(both_cores(grads_zero), both_cores(kept_zero), both_cores(grads_one), both_cores(kept_one))
    columns = [[2 * z + c for z in range(chips)] for c in range(2)]
    parts = lax.all_to_all(pair, "ctx", 0, 0, tiled=True, axis_index_groups=columns)
    grad_in, grad_out = call(total_kernel, [((1, LANE, G), f32), ((1, G, LANE), f32)])(parts)
    return (grad_in, grad_out)


def solution(mesh):
    placed = (
        P(("ctx", "exp"), None),
        P(("ctx", "exp"), None),
        P(None, ("ctx", "exp"), None),
        P("exp", "ctx", None),
        P("exp", None, "ctx"),
        P("ctx", "exp"),
    )
    return jax.shard_map(
        on_device,
        mesh=mesh,
        in_specs=placed,
        out_specs=(P("exp", "ctx", None), P("exp", None, "ctx")),
        check_vma=False,
    )
```

```python
import functools

import jax
import jax.numpy as jnp
from jax import lax
from jax.experimental import pallas as pl
from jax.experimental.pallas import tpu as pltpu
from jax.sharding import PartitionSpec as P

epsilon = 1e-06
TOK, D, G, EXPERTS, CAP = 128, 2048, 256, 32, 3
SLOTS = EXPERTS * CAP
LANE = 128
CHUNKS = D // LANE
PEER = CAP * CHUNKS
CHIPS = 8
SHARD = 2 * G + 16
bf16, f32 = jnp.bfloat16, jnp.float32


def iota(shape, dimension):
    return lax.broadcasted_iota(jnp.int32, shape, dimension)


def choose(ids):
    hit = iota((EXPERTS, TOK), 0) == ids
    earlier = jnp.where(iota((TOK, TOK), 0) < iota((TOK, TOK), 1), 1.0, 0.0).astype(bf16)
    before = jnp.dot(jnp.where(hit, 1.0, 0.0).astype(bf16), earlier, preferred_element_type=f32)
    position = jnp.sum(jnp.where(hit, before, 0.0), axis=0, keepdims=True).astype(jnp.int32)
    slot = jnp.where(position < CAP, position * EXPERTS + ids, -1)
    return jnp.where(iota((SLOTS, TOK), 0) == slot, 1.0, 0.0).astype(bf16)


def to_slots(pick, rows):
    return jnp.dot(pick, rows, preferred_element_type=f32)


def to_tokens(pick, rows):
    return lax.dot_general(pick, rows, (((0,), (0,)), ((), ())), preferred_element_type=f32)


def pack(rows, wide, stride=PEER, first=0):
    for r in range(CAP):
        for k in range(CHUNKS):
            wide[pl.ds(first + r * CHUNKS + k, EXPERTS, stride=stride), :] = rows[
                r * EXPERTS : (r + 1) * EXPERTS, k * LANE : (k + 1) * LANE
            ]


def unpack(wide, dense, stride=PEER, first=0):
    for r in range(CAP):
        for k in range(CHUNKS):
            dense[r * EXPERTS : (r + 1) * EXPERTS, k * LANE : (k + 1) * LANE] = wide[
                pl.ds(first + r * CHUNKS + k, EXPERTS, stride=stride), :
            ].astype(dense.dtype)


def normalize(state):
    scale = jnp.sqrt(jnp.mean(state * state, axis=-1, keepdims=True) + epsilon)
    return state / scale, scale


def share_kernel(weight_in, weight_out, router, out):
    out[:LANE, :] = weight_in[0, :, :LANE]
    out[LANE:G, :] = weight_in[0, :, LANE:]
    out[G : 2 * G, :] = weight_out[0]
    out[2 * G :, :] = jnp.broadcast_to(router[...], (SHARD - 2 * G, LANE))


def columns_kernel(own, pair_1, pair_2, column):
    chip = lax.div(lax.axis_index("ctx"), 2)
    column[...] = jnp.zeros_like(column)
    blocks = [(own, 0, chip)]
    for hop, pair in enumerate((pair_1, pair_2), 1):
        blocks += [(pair, 0, chip + CHIPS - hop), (pair, 2 * SHARD, chip + hop)]
    for block, first, where in blocks:
        for core in range(2):
            at = first + core * SHARD + 2 * G
            to = pl.multiple_of((2 * lax.rem(where, CHIPS) + core) * LANE, LANE)
            column[:, pl.ds(to, LANE)] = block[at : at + 1, :].astype(f32)


def place(block, first, chip, wa, wb, column):
    for core in range(2):
        at = first + core * SHARD
        to = pl.ds(pl.multiple_of((2 * chip + core) * LANE, LANE), LANE)
        wa[to, :LANE] = block[at : at + LANE, :]
        wa[to, LANE:] = block[at + LANE : at + G, :]
        wb[:, to] = block[at + G : at + 2 * G, :]
        column[:, to] = block[at + 2 * G : at + 2 * G + 1, :].astype(f32)


def split(full, narrow, own, mate, first=0):
    core = lax.rem(lax.axis_index("ctx"), 2)
    for z in range(CHIPS):
        to = slice(first + z * LANE, first + (z + 1) * LANE)
        own[:, to] = full[:, pl.ds(pl.multiple_of((2 * z + core) * LANE, LANE), LANE)]
        mate[:, to] = full[:, pl.ds(pl.multiple_of((2 * z + 1 - core) * LANE, LANE), LANE)]
    own[:, first + D // 2 : first + HALF] = narrow
    mate[:, first + D // 2 : first + HALF] = narrow


def forward(rows, wa, wb, column):
    before = jnp.dot(rows, wa[...], preferred_element_type=f32)
    positive = jnp.maximum(before, 0.0)
    hidden = (positive * positive).astype(bf16)
    expert_out = jnp.dot(hidden, wb[...], preferred_element_type=f32)
    logit = jnp.sum(rows.astype(f32) * column[...], axis=1, keepdims=True)
    gate = 1.0 / (1.0 + jnp.exp(-logit))
    return positive, hidden, expert_out, gate


def backward(upstream, wb, positive, gate):
    upper = upstream.astype(f32)
    grad_expert = (gate * upper).astype(bf16)
    grad_hidden = lax.dot_general(
        grad_expert, wb[...], (((1,), (1,)), ((), ())), preferred_element_type=f32
    )
    grad_pre = (grad_hidden * 2.0 * positive).astype(bf16)
    return upper, grad_expert, grad_pre


def dispatch_kernel(tokens, cotangent, ids, out, wide):
    unit, _ = normalize(tokens[...].astype(f32))
    pack(to_slots(choose(ids[0:1, :]), unit.astype(bf16)), wide, 2 * PEER, 0)
    pack(to_slots(choose(ids[1:2, :]), cotangent[...]), wide, 2 * PEER, PEER)
    out[...] = wide[...].astype(bf16)


def arrive_kernel(taken, rows, upstream, wide):
    wide[...] = taken[...].astype(f32)
    unpack(wide, rows, 2 * PEER, 0)
    unpack(wide, upstream, 2 * PEER, PEER)


def first_kernel(
    rows, own, pair_1, pair_2, pair_3, far, columns,
    out, positive_out, own_out, mate_out, gate_out, wa, wb, column, wide
):
    chip = lax.div(lax.axis_index("ctx"), 2)
    column[...] = columns[...]
    place(own, 0, chip, wa, wb, column)
    for hop, pair in enumerate((pair_1, pair_2, pair_3), 1):
        place(pair, 0, lax.rem(chip + CHIPS - hop, CHIPS), wa, wb, column)
        place(pair, 2 * SHARD, lax.rem(chip + hop, CHIPS), wa, wb, column)
    place(far, 0, lax.rem(chip + CHIPS // 2, CHIPS), wa, wb, column)
    positive, hidden, expert_out, gate = forward(rows[...], wa, wb, column)
    pack((gate * expert_out), wide)
    out[...] = wide[...].astype(bf16)
    positive_out[...] = positive
    split(rows, hidden, own_out, mate_out)
    gate_out[...] = jnp.broadcast_to(gate, (SLOTS, LANE))


def choose_kernel(ids, first, second):
    first[...] = choose(ids[0:1, :])
    second[...] = choose(ids[1:2, :])


def middle_kernel(tokens, pick_zero, pick_one, mixed, out, state_out, wide, dense):
    wide[...] = mixed[...].astype(f32)
    unpack(wide, dense)
    state = tokens[...].astype(f32) + to_tokens(pick_zero[...], dense[...])
    state_out[...] = state
    unit, _ = normalize(state)
    pack(to_slots(pick_one[...], unit.astype(bf16)), wide)
    out[...] = wide[...].astype(bf16)


def second_kernel(
    taken, upstream, wa, wb, column, out, own, mate, wide, dense, expert
):
    wide[...] = taken[...].astype(f32)
    unpack(wide, dense)
    positive, hidden, expert_out, gate = forward(dense[...], wa, wb, column)
    upper, grad_expert, grad_pre = backward(upstream[...], wb, positive, gate)
    grad_gate = jnp.sum(upper * expert_out, axis=1, keepdims=True)
    grad_logit = grad_gate * gate * (1.0 - gate)
    flowing = lax.dot_general(
        grad_pre, wa[...], (((1,), (1,)), ((), ())), preferred_element_type=f32
    )
    pack(flowing + grad_logit * column[...], wide)
    out[...] = wide[...].astype(bf16)
    expert[...] = grad_expert
    split(dense, hidden, own, mate)
    split(expert, grad_pre, own, mate, HALF)


def return_kernel(cotangent, state, pick_zero, pick_one, taken, out, wide, dense):
    wide[...] = taken[...].astype(f32)
    unpack(wide, dense)
    unit, scale = normalize(state[...])
    grad = to_tokens(pick_one[...], dense[...])
    inner = jnp.mean(grad * unit, axis=-1, keepdims=True)
    upstream = cotangent[...].astype(f32) + (grad - unit * inner) / scale
    pack(to_slots(pick_zero[...], upstream.astype(bf16)), wide)
    out[...] = wide[...].astype(bf16)


def over_rows(left, right):
    return lax.dot_general(left, right, (((0,), (0,)), ((), ())), preferred_element_type=f32)


def first_grad_kernel(taken, wb, positive, gate, own, mate, wide, dense):
    wide[...] = taken[...].astype(f32)
    unpack(wide, dense)
    _, grad_expert, grad_pre = backward(dense[...], wb, positive[...], gate[:, :1])
    dense[...] = grad_expert
    split(dense, grad_pre, own, mate)


def weight_kernel(
    grads_own, grads_both, kept_own, kept_mate, one_own, one_mate, out, rows, hidden, grads, pre
):
    mate = pl.multiple_of((1 - lax.rem(lax.axis_index("ctx"), 2)) * SLOTS, SLOTS)
    kept = (kept_own[...], kept_mate[...], one_own[:, :HALF], one_mate[:, :HALF])
    grad = (grads_own[...], grads_both[pl.ds(mate, SLOTS), :], one_own[:, HALF:], one_mate[:, HALF:])
    for i in range(4):
        to = slice(i * SLOTS, (i + 1) * SLOTS)
        rows[to, :], hidden[to, :] = kept[i][:, : D // 2], kept[i][:, D // 2 :]
        grads[to, :], pre[to, :] = grad[i][:, : D // 2], grad[i][:, D // 2 :]
    part_in = over_rows(pre[...], rows[...])
    part_out = over_rows(hidden[...], grads[...])
    for z in range(CHIPS):
        at = slice(z * LANE, (z + 1) * LANE)
        out[z, :G, :] = part_in[:, at].astype(bf16)
        out[z, G:, :] = part_out[:, at].astype(bf16)


def total_kernel(parts, grad_in, grad_out):
    total = parts[0].astype(f32)
    for z in range(1, CHIPS):
        total = total + parts[z].astype(f32)
    grad_in[0] = total[:G, :].T
    grad_out[0] = total[G:, :]


def call(kernel, outs, scratch=(), room=24, cost=0):
    return pl.pallas_call(
        kernel,
        out_shape=[jax.ShapeDtypeStruct(s, t) for s, t in outs],
        scratch_shapes=[pltpu.VMEM(s, t) for s, t in scratch],
        compiler_params=pltpu.CompilerParams(vmem_limit_bytes=room << 20),
        cost_estimate=pl.CostEstimate(flops=cost, bytes_accessed=0, transcendentals=0)
        if cost
        else None,
    )


PACKED = ((EXPERTS * PEER, LANE), bf16)
WIDE = ((EXPERTS * PEER, LANE), f32)
DENSE = ((SLOTS, D), bf16)
PICK = ((SLOTS, TOK), bf16)
HALF = D // 2 + G
KEPT = ((SLOTS, HALF), bf16)
WEIGHTS = (((D, G), bf16), ((G, D), bf16), ((1, D), f32))


def over_exp(buffer):
    shaped = buffer.reshape(EXPERTS, -1, LANE)
    return lax.all_to_all(shaped, "exp", 0, 0, tiled=True).reshape(buffer.shape)


def on_device(tokens, cotangent, expert_ids, weight_in, weight_out, router):
    chips = lax.axis_size("ctx") // 2
    ids = expert_ids[:, :, 0]
    cores = [[2 * z, 2 * z + 1] for z in range(chips)]

    def both_cores(value):
        return lax.all_gather(value, "ctx", axis=0, tiled=True, axis_index_groups=cores)

    around = [(2 * z, 2 * ((z + 1) % chips)) for z in range(chips)]
    around += [(2 * z + 1, 2 * ((z - 1) % chips) + 1) for z in range(chips)]
    (share,) = call(share_kernel, [((SHARD, LANE), bf16)], room=60)(
        weight_in, weight_out, router.reshape(1, LANE)
    )
    own = both_cores(share)
    wide_two = ((2 * EXPERTS * PEER, LANE), f32)
    (leaving,) = call(dispatch_kernel, [((2 * EXPERTS * PEER, LANE), bf16)], [wide_two], room=60)(
        tokens, cotangent, ids
    )
    passing = lax.ppermute(own, "ctx", around)
    leaving, passing = lax.optimization_barrier((leaving, passing))
    pairs = [passing]
    passing = lax.ppermute(passing, "ctx", around)
    pairs.append(passing)
    passing = lax.ppermute(passing, "ctx", around)
    pairs = [both_cores(pair) for pair in pairs]
    picks = call(choose_kernel, [PICK, PICK])(ids)
    passing, *rest = lax.optimization_barrier((passing, *pairs, *picks))
    pairs, picks = rest[:2], rest[2:]
    pairs += [both_cores(passing), lax.ppermute(passing, "ctx", around)]
    (columns,) = call(columns_kernel, [WEIGHTS[2]], cost=10 * 1150000000)(own, *pairs[:2])
    rows_zero, upstream_one = call(arrive_kernel, [DENSE, DENSE], [wide_two])(over_exp(leaving))
    mixed, positive, kept_own, kept_mate, gate, wa, wb, column = call(
        first_kernel,
        [PACKED, ((SLOTS, G), f32), KEPT, KEPT, ((SLOTS, LANE), f32), *WEIGHTS],
        [WIDE],
    )(rows_zero, own, *pairs, columns)
    across = [(2 * z + c, 2 * z + 1 - c) for z in range(chips) for c in range(2)]
    kept_mate = lax.ppermute(kept_mate, "ctx", across)
    leaving, state_one = call(middle_kernel, [PACKED, ((TOK, D), f32)], [WIDE, DENSE])(
        tokens, *picks, over_exp(mixed)
    )
    double = ((SLOTS, 2 * HALF), bf16)
    leaving, one_own, one_mate = call(
        second_kernel, [PACKED, double, double], [WIDE, DENSE, DENSE]
    )(over_exp(leaving), upstream_one, wa, wb, column)
    one_mate = lax.ppermute(one_mate, "ctx", across)
    (leaving,) = call(return_kernel, [PACKED], [WIDE, DENSE])(
        cotangent, state_one, *picks, over_exp(leaving)
    )
    grads_own, grads_mate = call(first_grad_kernel, [KEPT, KEPT], [WIDE, DENSE])(
        over_exp(leaving), wb, positive, gate
    )
    half, narrow = ((4 * SLOTS, D // 2), bf16), ((4 * SLOTS, G), bf16)
    (pair,) = call(
        weight_kernel, [((CHIPS, 2 * G, LANE), bf16)], [half, narrow, half, narrow]
    )(grads_own, both_cores(grads_mate), kept_own, kept_mate, one_own, one_mate)
    columns = [[2 * z + c for z in range(chips)] for c in range(2)]
    parts = lax.all_to_all(pair, "ctx", 0, 0, tiled=True, axis_index_groups=columns)
    grad_in, grad_out = call(total_kernel, [((1, LANE, G), f32), ((1, G, LANE), f32)])(parts)
    return (grad_in, grad_out)


def solution(mesh):
    placed = (
        P(("ctx", "exp"), None),
        P(("ctx", "exp"), None),
        P(None, ("ctx", "exp"), None),
        P("exp", "ctx", None),
        P("exp", None, "ctx"),
        P("ctx", "exp"),
    )
    return jax.shard_map(
        on_device,
        mesh=mesh,
        in_specs=placed,
        out_specs=(P("exp", "ctx", None), P("exp", None, "ctx")),
        check_vma=False,
    )
```

```python
import functools

import jax
import jax.numpy as jnp
from jax import lax
from jax.experimental import pallas as pl
from jax.experimental.pallas import tpu as pltpu
from jax.sharding import PartitionSpec as P

epsilon = 1e-06
TOK, D, G, EXPERTS, CAP = 128, 2048, 256, 32, 3
SLOTS = EXPERTS * CAP
LANE = 128
CHUNKS = D // LANE
PEER = CAP * CHUNKS
CHIPS = 8
SHARD = 2 * G + 16
bf16, f32 = jnp.bfloat16, jnp.float32


def iota(shape, dimension):
    return lax.broadcasted_iota(jnp.int32, shape, dimension)


def choose(ids):
    hit = iota((EXPERTS, TOK), 0) == ids
    earlier = jnp.where(iota((TOK, TOK), 0) < iota((TOK, TOK), 1), 1.0, 0.0).astype(bf16)
    before = jnp.dot(jnp.where(hit, 1.0, 0.0).astype(bf16), earlier, preferred_element_type=f32)
    position = jnp.sum(jnp.where(hit, before, 0.0), axis=0, keepdims=True).astype(jnp.int32)
    slot = jnp.where(position < CAP, position * EXPERTS + ids, -1)
    return jnp.where(iota((SLOTS, TOK), 0) == slot, 1.0, 0.0).astype(bf16)


def to_slots(pick, rows):
    return jnp.dot(pick, rows, preferred_element_type=f32)


def to_tokens(pick, rows):
    return lax.dot_general(pick, rows, (((0,), (0,)), ((), ())), preferred_element_type=f32)


def pack(rows, wide, stride=PEER, first=0):
    for r in range(CAP):
        for k in range(CHUNKS):
            wide[pl.ds(first + r * CHUNKS + k, EXPERTS, stride=stride), :] = rows[
                r * EXPERTS : (r + 1) * EXPERTS, k * LANE : (k + 1) * LANE
            ]


def unpack(wide, dense, stride=PEER, first=0):
    for r in range(CAP):
        for k in range(CHUNKS):
            dense[r * EXPERTS : (r + 1) * EXPERTS, k * LANE : (k + 1) * LANE] = wide[
                pl.ds(first + r * CHUNKS + k, EXPERTS, stride=stride), :
            ].astype(dense.dtype)


def normalize(state):
    scale = jnp.sqrt(jnp.mean(state * state, axis=-1, keepdims=True) + epsilon)
    return state / scale, scale


def share_kernel(weight_in, weight_out, router, out):
    out[:LANE, :] = weight_in[0, :, :LANE]
    out[LANE:G, :] = weight_in[0, :, LANE:]
    out[G : 2 * G, :] = weight_out[0]
    out[2 * G :, :] = jnp.broadcast_to(router[...], (SHARD - 2 * G, LANE))


def columns_kernel(own, pair_1, pair_2, column):
    chip = lax.div(lax.axis_index("ctx"), 2)
    column[...] = jnp.zeros_like(column)
    blocks = [(own, 0, chip)]
    for hop, pair in enumerate((pair_1, pair_2), 1):
        blocks += [(pair, 0, chip + CHIPS - hop), (pair, 2 * SHARD, chip + hop)]
    for block, first, where in blocks:
        for core in range(2):
            at = first + core * SHARD + 2 * G
            to = pl.multiple_of((2 * lax.rem(where, CHIPS) + core) * LANE, LANE)
            column[:, pl.ds(to, LANE)] = block[at : at + 1, :].astype(f32)


def place(block, first, chip, wa, wb, column):
    for core in range(2):
        at = first + core * SHARD
        to = pl.ds(pl.multiple_of((2 * chip + core) * LANE, LANE), LANE)
        wa[to, :LANE] = block[at : at + LANE, :]
        wa[to, LANE:] = block[at + LANE : at + G, :]
        wb[:, to] = block[at + G : at + 2 * G, :]
        column[:, to] = block[at + 2 * G : at + 2 * G + 1, :].astype(f32)


def own_chunks(core):
    chip = lax.div(lax.axis_index("ctx"), 2)
    way = 1 - 2 * core

    def chunk(hops, parity):
        return 2 * lax.rem(chip + hops * way + CHIPS, CHIPS) + parity

    pairs = [chunk(hops, parity) for hops in (1, 3, 2) for parity in range(2)]
    return pairs[:4] + [chunk(4, core)] + pairs[4:] + [chunk(0, core)]


def split(full, narrow, own, mate, first=0):
    core = lax.rem(lax.axis_index("ctx"), 2)
    for half, chunks in ((own, own_chunks(core)), (mate, own_chunks(1 - core))):
        for i, chunk in enumerate(chunks):
            at = pl.ds(pl.multiple_of(chunk * LANE, LANE), LANE)
            half[:, first + i * LANE : first + (i + 1) * LANE] = full[:, at]
        half[:, first + D // 2 : first + HALF] = narrow


def forward(rows, wa, wb, column):
    before = jnp.dot(rows, wa[...], preferred_element_type=f32)
    positive = jnp.maximum(before, 0.0)
    hidden = (positive * positive).astype(bf16)
    expert_out = jnp.dot(hidden, wb[...], preferred_element_type=f32)
    logit = jnp.sum(rows.astype(f32) * column[...], axis=1, keepdims=True)
    gate = 1.0 / (1.0 + jnp.exp(-logit))
    return positive, hidden, expert_out, gate


def backward(upstream, wb, positive, gate):
    upper = upstream.astype(f32)
    grad_expert = (gate * upper).astype(bf16)
    grad_hidden = lax.dot_general(
        grad_expert, wb[...], (((1,), (1,)), ((), ())), preferred_element_type=f32
    )
    grad_pre = (grad_hidden * 2.0 * positive).astype(bf16)
    return upper, grad_expert, grad_pre


def dispatch_kernel(tokens, cotangent, ids, out, wide):
    unit, _ = normalize(tokens[...].astype(f32))
    pack(to_slots(choose(ids[0:1, :]), unit.astype(bf16)), wide, 2 * PEER, 0)
    pack(to_slots(choose(ids[1:2, :]), cotangent[...]), wide, 2 * PEER, PEER)
    out[...] = wide[...].astype(bf16)


def arrive_kernel(taken, rows, upstream, wide):
    wide[...] = taken[...].astype(f32)
    unpack(wide, rows, 2 * PEER, 0)
    unpack(wide, upstream, 2 * PEER, PEER)


def first_kernel(
    rows, own, pair_1, pair_2, pair_3, far, columns,
    out, positive_out, own_out, mate_out, gate_out, wa, wb, column, wide
):
    chip = lax.div(lax.axis_index("ctx"), 2)
    column[...] = columns[...]
    place(own, 0, chip, wa, wb, column)
    for hop, pair in enumerate((pair_1, pair_2, pair_3), 1):
        place(pair, 0, lax.rem(chip + CHIPS - hop, CHIPS), wa, wb, column)
        place(pair, 2 * SHARD, lax.rem(chip + hop, CHIPS), wa, wb, column)
    place(far, 0, lax.rem(chip + CHIPS // 2, CHIPS), wa, wb, column)
    positive, hidden, expert_out, gate = forward(rows[...], wa, wb, column)
    pack((gate * expert_out), wide)
    out[...] = wide[...].astype(bf16)
    positive_out[...] = positive
    split(rows, hidden, own_out, mate_out)
    gate_out[...] = jnp.broadcast_to(gate, (SLOTS, LANE))


def choose_kernel(ids, first, second):
    first[...] = choose(ids[0:1, :])
    second[...] = choose(ids[1:2, :])


def middle_kernel(tokens, pick_zero, pick_one, mixed, out, state_out, wide, dense):
    wide[...] = mixed[...].astype(f32)
    unpack(wide, dense)
    state = tokens[...].astype(f32) + to_tokens(pick_zero[...], dense[...])
    state_out[...] = state
    unit, _ = normalize(state)
    pack(to_slots(pick_one[...], unit.astype(bf16)), wide)
    out[...] = wide[...].astype(bf16)


def second_kernel(
    taken, upstream, wa, wb, column, out, own, mate, wide, dense, expert
):
    wide[...] = taken[...].astype(f32)
    unpack(wide, dense)
    positive, hidden, expert_out, gate = forward(dense[...], wa, wb, column)
    upper, grad_expert, grad_pre = backward(upstream[...], wb, positive, gate)
    grad_gate = jnp.sum(upper * expert_out, axis=1, keepdims=True)
    grad_logit = grad_gate * gate * (1.0 - gate)
    flowing = lax.dot_general(
        grad_pre, wa[...], (((1,), (1,)), ((), ())), preferred_element_type=f32
    )
    pack(flowing + grad_logit * column[...], wide)
    out[...] = wide[...].astype(bf16)
    expert[...] = grad_expert
    split(dense, hidden, own, mate)
    split(expert, grad_pre, own, mate, HALF)


def return_kernel(cotangent, state, pick_zero, pick_one, taken, out, wide, dense):
    wide[...] = taken[...].astype(f32)
    unpack(wide, dense)
    unit, scale = normalize(state[...])
    grad = to_tokens(pick_one[...], dense[...])
    inner = jnp.mean(grad * unit, axis=-1, keepdims=True)
    upstream = cotangent[...].astype(f32) + (grad - unit * inner) / scale
    pack(to_slots(pick_zero[...], upstream.astype(bf16)), wide)
    out[...] = wide[...].astype(bf16)


def over_rows(left, right):
    return lax.dot_general(left, right, (((0,), (0,)), ((), ())), preferred_element_type=f32)


def first_grad_kernel(taken, wb, positive, gate, own, mate, wide, dense):
    wide[...] = taken[...].astype(f32)
    unpack(wide, dense)
    _, grad_expert, grad_pre = backward(dense[...], wb, positive[...], gate[:, :1])
    dense[...] = grad_expert
    split(dense, grad_pre, own, mate)


def weight_kernel(
    grads_own, grads_both, kept_own, kept_mate, one_own, one_mate,
    near, far, next_chip, own_chip, rows, hidden, grads, pre
):
    mate = pl.multiple_of((1 - lax.rem(lax.axis_index("ctx"), 2)) * SLOTS, SLOTS)
    kept = (kept_own[...], kept_mate[...], one_own[:, :HALF], one_mate[:, :HALF])
    grad = (grads_own[...], grads_both[pl.ds(mate, SLOTS), :], one_own[:, HALF:], one_mate[:, HALF:])
    for i in range(4):
        to = slice(i * SLOTS, (i + 1) * SLOTS)
        rows[to, :], hidden[to, :] = kept[i][:, : D // 2], kept[i][:, D // 2 :]
        grads[to, :], pre[to, :] = grad[i][:, : D // 2], grad[i][:, D // 2 :]
    part_in = over_rows(pre[...], rows[...])
    part_out = over_rows(hidden[...], grads[...])
    targets = [(near, i) for i in range(4)] + [(far, 0), (next_chip, 0), (next_chip, 1), (own_chip, 0)]
    for i, (out, to) in enumerate(targets):
        at = slice(i * LANE, (i + 1) * LANE)
        out[to, :G, :] = part_in[:, at].astype(out.dtype)
        out[to, G:, :] = part_out[:, at].astype(out.dtype)


def relay_kernel(near, far, next_chip, same, cross, give):
    core = lax.rem(lax.axis_index("ctx"), 2)
    same[...] = (
        next_chip[core] + near[2 + core].astype(f32) + far[0].astype(f32)
    ).astype(bf16)
    cross[...] = (next_chip[1 - core] + near[3 - core].astype(f32)).astype(bf16)
    give[...] = near[1 - core]


def total_kernel(own_chip, near, gives, same, cross, grad_in, grad_out):
    core = lax.rem(lax.axis_index("ctx"), 2)
    mate = pl.multiple_of((1 - core) * 2 * G, 2 * G)
    total = own_chip[0] + near[core].astype(f32) + gives[pl.ds(mate, 2 * G), :].astype(f32)
    total = total + same[...].astype(f32) + cross[...].astype(f32)
    grad_in[0] = total[:G, :].T
    grad_out[0] = total[G:, :]


def call(kernel, outs, scratch=(), room=24, cost=0):
    return pl.pallas_call(
        kernel,
        out_shape=[jax.ShapeDtypeStruct(s, t) for s, t in outs],
        scratch_shapes=[pltpu.VMEM(s, t) for s, t in scratch],
        compiler_params=pltpu.CompilerParams(vmem_limit_bytes=room << 20),
        cost_estimate=pl.CostEstimate(flops=cost, bytes_accessed=0, transcendentals=0)
        if cost
        else None,
    )


PACKED = ((EXPERTS * PEER, LANE), bf16)
WIDE = ((EXPERTS * PEER, LANE), f32)
DENSE = ((SLOTS, D), bf16)
PICK = ((SLOTS, TOK), bf16)
HALF = D // 2 + G
KEPT = ((SLOTS, HALF), bf16)
WEIGHTS = (((D, G), bf16), ((G, D), bf16), ((1, D), f32))


def over_exp(buffer):
    shaped = buffer.reshape(EXPERTS, -1, LANE)
    return lax.all_to_all(shaped, "exp", 0, 0, tiled=True).reshape(buffer.shape)


def on_device(tokens, cotangent, expert_ids, weight_in, weight_out, router):
    chips = lax.axis_size("ctx") // 2
    ids = expert_ids[:, :, 0]
    cores = [[2 * z, 2 * z + 1] for z in range(chips)]

    def both_cores(value):
        return lax.all_gather(value, "ctx", axis=0, tiled=True, axis_index_groups=cores)

    around = [(2 * z, 2 * ((z + 1) % chips)) for z in range(chips)]
    around += [(2 * z + 1, 2 * ((z - 1) % chips) + 1) for z in range(chips)]
    (share,) = call(share_kernel, [((SHARD, LANE), bf16)], room=60)(
        weight_in, weight_out, router.reshape(1, LANE)
    )
    own = both_cores(share)
    wide_two = ((2 * EXPERTS * PEER, LANE), f32)
    (leaving,) = call(dispatch_kernel, [((2 * EXPERTS * PEER, LANE), bf16)], [wide_two], room=60)(
        tokens, cotangent, ids
    )
    two_on = [
        (2 * z + c, 2 * ((z + 2 - 4 * c) % chips) + c) for z in range(chips) for c in range(2)
    ]
    one, two = lax.ppermute(own, "ctx", around), lax.ppermute(own, "ctx", two_on)
    _, two = lax.optimization_barrier((leaving, two))
    three, four = lax.ppermute(two, "ctx", around), lax.ppermute(two, "ctx", two_on)
    pairs = [both_cores(one), both_cores(two), both_cores(three), four]
    picks = call(choose_kernel, [PICK, PICK])(ids)
    (columns,) = call(columns_kernel, [WEIGHTS[2]], cost=10 * 1150000000)(own, *pairs[:2])
    columns, picks = lax.optimization_barrier((columns, picks))
    rows_zero, upstream_one = call(arrive_kernel, [DENSE, DENSE], [wide_two])(over_exp(leaving))
    mixed, positive, kept_own, kept_mate, gate, wa, wb, column = call(
        first_kernel,
        [PACKED, ((SLOTS, G), f32), KEPT, KEPT, ((SLOTS, LANE), f32), *WEIGHTS],
        [WIDE],
    )(rows_zero, own, *pairs, columns)
    across = [(2 * z + c, 2 * z + 1 - c) for z in range(chips) for c in range(2)]
    kept_mate = lax.ppermute(kept_mate, "ctx", across)
    leaving, state_one = call(middle_kernel, [PACKED, ((TOK, D), f32)], [WIDE, DENSE])(
        tokens, *picks, over_exp(mixed)
    )
    double = ((SLOTS, 2 * HALF), bf16)
    leaving, one_own, one_mate = call(
        second_kernel, [PACKED, double, double], [WIDE, DENSE, DENSE]
    )(over_exp(leaving), upstream_one, wa, wb, column)
    one_mate = lax.ppermute(one_mate, "ctx", across)
    (leaving,) = call(return_kernel, [PACKED], [WIDE, DENSE])(
        cotangent, state_one, *picks, over_exp(leaving)
    )
    grads_own, grads_mate = call(first_grad_kernel, [KEPT, KEPT], [WIDE, DENSE])(
        over_exp(leaving), wb, positive, gate
    )
    half, narrow = ((4 * SLOTS, D // 2), bf16), ((4 * SLOTS, G), bf16)
    chunk = (2 * G, LANE)
    near, far, next_chip, own_chip = call(
        weight_kernel,
        [((4, *chunk), bf16), ((1, *chunk), bf16), ((2, *chunk), f32), ((1, *chunk), f32)],
        [half, narrow, half, narrow],
    )(grads_own, both_cores(grads_mate), kept_own, kept_mate, one_own, one_mate)
    near, far = lax.ppermute(near, "ctx", around), lax.ppermute(far, "ctx", two_on)
    same, cross, give = call(relay_kernel, [(chunk, bf16)] * 3)(near, far, next_chip)
    same = lax.ppermute(same, "ctx", two_on)
    cross = lax.ppermute(cross, "ctx", [(a, b + 1 - 2 * (b % 2)) for a, b in two_on])
    grad_in, grad_out = call(total_kernel, [((1, LANE, G), f32), ((1, G, LANE), f32)])(
        own_chip, near, both_cores(give), same, cross
    )
    return (grad_in, grad_out)


def solution(mesh):
    placed = (
        P(("ctx", "exp"), None),
        P(("ctx", "exp"), None),
        P(None, ("ctx", "exp"), None),
        P("exp", "ctx", None),
        P("exp", None, "ctx"),
        P("ctx", "exp"),
    )
    return jax.shard_map(
        on_device,
        mesh=mesh,
        in_specs=placed,
        out_specs=(P("exp", "ctx", None), P("exp", None, "ctx")),
        check_vma=False,
    )
```

```python
import functools

import jax
import jax.numpy as jnp
from jax import lax
from jax.experimental import pallas as pl
from jax.experimental.pallas import tpu as pltpu
from jax.sharding import PartitionSpec as P

epsilon = 1e-06
TOK, D, G, EXPERTS, CAP = 128, 2048, 256, 32, 3
SLOTS = EXPERTS * CAP
LANE = 128
CHUNKS = D // LANE
PEER = CAP * CHUNKS
CHIPS = 8
SHARD = 2 * G + 16
bf16, f32 = jnp.bfloat16, jnp.float32


def iota(shape, dimension):
    return lax.broadcasted_iota(jnp.int32, shape, dimension)


def choose(ids):
    hit = iota((EXPERTS, TOK), 0) == ids
    earlier = jnp.where(iota((TOK, TOK), 0) < iota((TOK, TOK), 1), 1.0, 0.0).astype(bf16)
    before = jnp.dot(jnp.where(hit, 1.0, 0.0).astype(bf16), earlier, preferred_element_type=f32)
    position = jnp.sum(jnp.where(hit, before, 0.0), axis=0, keepdims=True).astype(jnp.int32)
    slot = jnp.where(position < CAP, position * EXPERTS + ids, -1)
    return jnp.where(iota((SLOTS, TOK), 0) == slot, 1.0, 0.0).astype(bf16)


def to_slots(pick, rows):
    return jnp.dot(pick, rows, preferred_element_type=f32)


def to_tokens(pick, rows):
    return lax.dot_general(pick, rows, (((0,), (0,)), ((), ())), preferred_element_type=f32)


def pack(rows, wide, stride=PEER, first=0):
    for r in range(CAP):
        for k in range(CHUNKS):
            wide[pl.ds(first + r * CHUNKS + k, EXPERTS, stride=stride), :] = rows[
                r * EXPERTS : (r + 1) * EXPERTS, k * LANE : (k + 1) * LANE
            ]


def unpack(wide, dense, stride=PEER, first=0):
    for r in range(CAP):
        for k in range(CHUNKS):
            dense[r * EXPERTS : (r + 1) * EXPERTS, k * LANE : (k + 1) * LANE] = wide[
                pl.ds(first + r * CHUNKS + k, EXPERTS, stride=stride), :
            ].astype(dense.dtype)


def normalize(state):
    scale = jnp.sqrt(jnp.mean(state * state, axis=-1, keepdims=True) + epsilon)
    return state / scale, scale


def share_kernel(weight_in, weight_out, router, out):
    out[:LANE, :] = weight_in[0, :, :LANE]
    out[LANE:G, :] = weight_in[0, :, LANE:]
    out[G : 2 * G, :] = weight_out[0]
    out[2 * G :, :] = jnp.broadcast_to(router[...], (SHARD - 2 * G, LANE))


def columns_kernel(own, pair_1, pair_2, column):
    chip = lax.div(lax.axis_index("ctx"), 2)
    column[...] = jnp.zeros_like(column)
    blocks = [(own, 0, chip)]
    for hop, pair in enumerate((pair_1, pair_2), 1):
        blocks += [(pair, 0, chip + CHIPS - hop), (pair, 2 * SHARD, chip + hop)]
    for block, first, where in blocks:
        for core in range(2):
            at = first + core * SHARD + 2 * G
            to = pl.multiple_of((2 * lax.rem(where, CHIPS) + core) * LANE, LANE)
            column[:, pl.ds(to, LANE)] = block[at : at + 1, :].astype(f32)


def place(block, first, chip, wa, wb, column):
    for core in range(2):
        at = first + core * SHARD
        to = pl.ds(pl.multiple_of((2 * chip + core) * LANE, LANE), LANE)
        wa[to, :LANE] = block[at : at + LANE, :]
        wa[to, LANE:] = block[at + LANE : at + G, :]
        wb[:, to] = block[at + G : at + 2 * G, :]
        column[:, to] = block[at + 2 * G : at + 2 * G + 1, :].astype(f32)


def own_chunks(core):
    chip = lax.div(lax.axis_index("ctx"), 2)
    way = 1 - 2 * core

    def chunk(hops, parity):
        return 2 * lax.rem(chip + hops * way + CHIPS, CHIPS) + parity

    pairs = [chunk(hops, parity) for hops in (1, 3, 2) for parity in range(2)]
    return pairs[:4] + [chunk(4, core)] + pairs[4:] + [chunk(0, core)]


def split(full, narrow, own, mate, first=0):
    core = lax.rem(lax.axis_index("ctx"), 2)
    for half, chunks in ((own, own_chunks(core)), (mate, own_chunks(1 - core))):
        for i, chunk in enumerate(chunks):
            at = pl.ds(pl.multiple_of(chunk * LANE, LANE), LANE)
            half[:, first + i * LANE : first + (i + 1) * LANE] = full[:, at]
        half[:, first + D // 2 : first + HALF] = narrow


def forward(rows, wa, wb, column):
    before = jnp.dot(rows, wa[...], preferred_element_type=f32)
    positive = jnp.maximum(before, 0.0)
    hidden = (positive * positive).astype(bf16)
    expert_out = jnp.dot(hidden, wb[...], preferred_element_type=f32)
    logit = jnp.sum(rows.astype(f32) * column[...], axis=1, keepdims=True)
    gate = 1.0 / (1.0 + jnp.exp(-logit))
    return positive, hidden, expert_out, gate


def backward(upstream, wb, positive, gate):
    upper = upstream.astype(f32)
    grad_expert = (gate * upper).astype(bf16)
    grad_hidden = lax.dot_general(
        grad_expert, wb[...], (((1,), (1,)), ((), ())), preferred_element_type=f32
    )
    grad_pre = (grad_hidden * 2.0 * positive).astype(bf16)
    return upper, grad_expert, grad_pre


def dispatch_kernel(tokens, cotangent, ids, out, first, second, wide, packed, sems):
    loads = []
    for i, (source, target) in enumerate(((tokens, first), (cotangent, second))):
        for j in range(4):
            rows = pl.ds(j * TOK // 4, TOK // 4)
            copy = pltpu.make_async_copy(source.at[rows, :], target.at[rows, :], sems.at[4 * i + j])
            copy.start()
            loads.append(copy)
    picks = choose(ids[0:1, :]), choose(ids[1:2, :])
    stores = []
    for i in range(2):
        for copy in loads[4 * i : 4 * i + 4]:
            copy.wait()
        rows = second[...] if i else normalize(first[...].astype(f32))[0].astype(bf16)
        pack(to_slots(picks[i], rows), wide.at[i])
        packed[i] = wide[i].reshape(EXPERTS, PEER, LANE).astype(bf16)
        copy = pltpu.make_async_copy(
            packed.at[i], out.at[:, pl.ds(i * PEER, PEER), :], sems.at[8 + i]
        )
        copy.start()
        stores.append(copy)
    for copy in stores:
        copy.wait()


def arrive_kernel(taken, rows, upstream, wide):
    wide[...] = taken[...].astype(f32)
    unpack(wide, rows, 2 * PEER, 0)
    unpack(wide, upstream, 2 * PEER, PEER)


def first_kernel(
    rows, own, pair_1, pair_2, pair_3, far, columns,
    out, positive_out, own_out, mate_out, gate_out, wa, wb, column, wide
):
    chip = lax.div(lax.axis_index("ctx"), 2)
    column[...] = columns[...]
    place(own, 0, chip, wa, wb, column)
    for hop, pair in enumerate((pair_1, pair_2, pair_3), 1):
        place(pair, 0, lax.rem(chip + CHIPS - hop, CHIPS), wa, wb, column)
        place(pair, 2 * SHARD, lax.rem(chip + hop, CHIPS), wa, wb, column)
    place(far, 0, lax.rem(chip + CHIPS // 2, CHIPS), wa, wb, column)
    positive, hidden, expert_out, gate = forward(rows[...], wa, wb, column)
    pack((gate * expert_out), wide)
    out[...] = wide[...].astype(bf16)
    positive_out[...] = positive
    split(rows, hidden, own_out, mate_out)
    gate_out[...] = jnp.broadcast_to(gate, (SLOTS, LANE))


def choose_kernel(ids, first, second):
    first[...] = choose(ids[0:1, :])
    second[...] = choose(ids[1:2, :])


def middle_kernel(tokens, pick_zero, pick_one, mixed, out, state_out, wide, dense):
    wide[...] = mixed[...].astype(f32)
    unpack(wide, dense)
    state = tokens[...].astype(f32) + to_tokens(pick_zero[...], dense[...])
    state_out[...] = state
    unit, _ = normalize(state)
    pack(to_slots(pick_one[...], unit.astype(bf16)), wide)
    out[...] = wide[...].astype(bf16)


def second_kernel(
    taken, upstream, wa, wb, column, out, rows, hidden_out, expert, pre, wide
):
    wide[...] = taken[...].astype(f32)
    unpack(wide, rows)
    positive, hidden, expert_out, gate = forward(rows[...], wa, wb, column)
    upper, grad_expert, grad_pre = backward(upstream[...], wb, positive, gate)
    grad_gate = jnp.sum(upper * expert_out, axis=1, keepdims=True)
    grad_logit = grad_gate * gate * (1.0 - gate)
    flowing = lax.dot_general(
        grad_pre, wa[...], (((1,), (1,)), ((), ())), preferred_element_type=f32
    )
    pack(flowing + grad_logit * column[...], wide)
    out[...] = wide[...].astype(bf16)
    hidden_out[...] = hidden
    expert[...] = grad_expert
    pre[...] = grad_pre


def split_kernel(rows, hidden, expert, pre, own, mate):
    split(rows, hidden[...], own, mate)
    split(expert, pre[...], own, mate, HALF)


def return_kernel(cotangent, state, pick_zero, pick_one, taken, out, wide, dense):
    wide[...] = taken[...].astype(f32)
    unpack(wide, dense)
    unit, scale = normalize(state[...])
    grad = to_tokens(pick_one[...], dense[...])
    inner = jnp.mean(grad * unit, axis=-1, keepdims=True)
    upstream = cotangent[...].astype(f32) + (grad - unit * inner) / scale
    pack(to_slots(pick_zero[...], upstream.astype(bf16)), wide)
    out[...] = wide[...].astype(bf16)


def over_rows(left, right):
    return lax.dot_general(left, right, (((0,), (0,)), ((), ())), preferred_element_type=f32)


def first_grad_kernel(taken, wb, positive, gate, own, mate, wide, dense):
    wide[...] = taken[...].astype(f32)
    unpack(wide, dense)
    _, grad_expert, grad_pre = backward(dense[...], wb, positive[...], gate[:, :1])
    dense[...] = grad_expert
    split(dense, grad_pre, own, mate)


def weight_kernel(
    grads_own, grads_both, kept_own, kept_mate, one_own, one_mate,
    near, far, next_chip, own_chip, rows, hidden, grads, pre
):
    mate = pl.multiple_of((1 - lax.rem(lax.axis_index("ctx"), 2)) * SLOTS, SLOTS)
    kept = (kept_own[...], kept_mate[...], one_own[:, :HALF], one_mate[:, :HALF])
    grad = (grads_own[...], grads_both[pl.ds(mate, SLOTS), :], one_own[:, HALF:], one_mate[:, HALF:])
    for i in range(4):
        to = slice(i * SLOTS, (i + 1) * SLOTS)
        rows[to, :], hidden[to, :] = kept[i][:, : D // 2], kept[i][:, D // 2 :]
        grads[to, :], pre[to, :] = grad[i][:, : D // 2], grad[i][:, D // 2 :]
    part_in = over_rows(pre[...], rows[...])
    part_out = over_rows(hidden[...], grads[...])
    targets = [(near, i) for i in range(4)] + [(far, 0), (next_chip, 0), (next_chip, 1), (own_chip, 0)]
    for i, (out, to) in enumerate(targets):
        at = slice(i * LANE, (i + 1) * LANE)
        out[to, :G, :] = part_in[:, at].astype(out.dtype)
        out[to, G:, :] = part_out[:, at].astype(out.dtype)


def relay_kernel(near, far, next_chip, same, cross, give):
    core = lax.rem(lax.axis_index("ctx"), 2)
    same[...] = (
        next_chip[core] + near[2 + core].astype(f32) + far[0].astype(f32)
    ).astype(bf16)
    cross[...] = (next_chip[1 - core] + near[3 - core].astype(f32)).astype(bf16)
    give[...] = near[1 - core]


def total_kernel(own_chip, near, gives, same, cross, grad_in, grad_out):
    core = lax.rem(lax.axis_index("ctx"), 2)
    mate = pl.multiple_of((1 - core) * 2 * G, 2 * G)
    total = own_chip[0] + near[core].astype(f32) + gives[pl.ds(mate, 2 * G), :].astype(f32)
    total = total + same[...].astype(f32) + cross[...].astype(f32)
    grad_in[0] = total[:G, :].T
    grad_out[0] = total[G:, :]


def call(kernel, outs, scratch=(), room=24, cost=0):
    return pl.pallas_call(
        kernel,
        out_shape=[jax.ShapeDtypeStruct(s, t) for s, t in outs],
        scratch_shapes=[pltpu.VMEM(s, t) for s, t in scratch],
        compiler_params=pltpu.CompilerParams(vmem_limit_bytes=room << 20),
        cost_estimate=pl.CostEstimate(flops=cost, bytes_accessed=0, transcendentals=0)
        if cost
        else None,
    )


PACKED = ((EXPERTS * PEER, LANE), bf16)
WIDE = ((EXPERTS * PEER, LANE), f32)
DENSE = ((SLOTS, D), bf16)
PICK = ((SLOTS, TOK), bf16)
HALF = D // 2 + G
KEPT = ((SLOTS, HALF), bf16)
WEIGHTS = (((D, G), bf16), ((G, D), bf16), ((1, D), f32))


def over_exp(buffer):
    shaped = buffer.reshape(EXPERTS, -1, LANE)
    return lax.all_to_all(shaped, "exp", 0, 0, tiled=True).reshape(buffer.shape)


def on_device(tokens, cotangent, expert_ids, weight_in, weight_out, router):
    chips = lax.axis_size("ctx") // 2
    ids = expert_ids[:, :, 0]
    cores = [[2 * z, 2 * z + 1] for z in range(chips)]

    def both_cores(value):
        return lax.all_gather(value, "ctx", axis=0, tiled=True, axis_index_groups=cores)

    around = [(2 * z, 2 * ((z + 1) % chips)) for z in range(chips)]
    around += [(2 * z + 1, 2 * ((z - 1) % chips) + 1) for z in range(chips)]
    (share,) = call(share_kernel, [((SHARD, LANE), bf16)], room=60)(
        weight_in, weight_out, router.reshape(1, LANE)
    )
    own = both_cores(share)
    wide_two = ((2 * EXPERTS * PEER, LANE), f32)
    far_away = pl.BlockSpec(memory_space=pl.ANY)
    leaving = pl.pallas_call(
        dispatch_kernel,
        out_shape=jax.ShapeDtypeStruct((EXPERTS, 2 * PEER, LANE), bf16),
        in_specs=[far_away, far_away, pl.BlockSpec(memory_space=pltpu.VMEM)],
        out_specs=far_away,
        scratch_shapes=[
            pltpu.VMEM((TOK, D), bf16),
            pltpu.VMEM((TOK, D), bf16),
            pltpu.VMEM((2, EXPERTS * PEER, LANE), f32),
            pltpu.VMEM((2, EXPERTS, PEER, LANE), bf16),
            pltpu.SemaphoreType.DMA((10,)),
        ],
        compiler_params=pltpu.CompilerParams(vmem_limit_bytes=60 << 20),
    )(tokens, cotangent, ids).reshape(2 * EXPERTS * PEER, LANE)
    two_on = [
        (2 * z + c, 2 * ((z + 2 - 4 * c) % chips) + c) for z in range(chips) for c in range(2)
    ]
    two = lax.ppermute(own, "ctx", two_on)
    later, two = lax.optimization_barrier((own, two))
    _, two = lax.optimization_barrier((leaving, two))
    one = lax.ppermute(later, "ctx", around)
    three, four = lax.ppermute(two, "ctx", around), lax.ppermute(two, "ctx", two_on)
    pairs = [both_cores(one), both_cores(two), both_cores(three), four]
    picks = call(choose_kernel, [PICK, PICK])(ids)
    (columns,) = call(columns_kernel, [WEIGHTS[2]], cost=8 * 1150000000)(own, *pairs[:2])
    columns, picks = lax.optimization_barrier((columns, picks))
    rows_zero, upstream_one = call(arrive_kernel, [DENSE, DENSE], [wide_two])(over_exp(leaving))
    mixed, positive, kept_own, kept_mate, gate, wa, wb, column = call(
        first_kernel,
        [PACKED, ((SLOTS, G), f32), KEPT, KEPT, ((SLOTS, LANE), f32), *WEIGHTS],
        [WIDE],
    )(rows_zero, own, *pairs, columns)
    across = [(2 * z + c, 2 * z + 1 - c) for z in range(chips) for c in range(2)]
    kept_mate = lax.ppermute(kept_mate, "ctx", across)
    leaving, state_one = call(middle_kernel, [PACKED, ((TOK, D), f32)], [WIDE, DENSE])(
        tokens, *picks, over_exp(mixed)
    )
    double = ((SLOTS, 2 * HALF), bf16)
    slim = ((SLOTS, G), bf16)
    leaving, *second = call(second_kernel, [PACKED, DENSE, slim, DENSE, slim], [WIDE])(
        over_exp(leaving), upstream_one, wa, wb, column
    )
    one_own, one_mate = call(split_kernel, [double, double])(*second)
    one_mate = lax.ppermute(one_mate, "ctx", across)
    (leaving,) = call(return_kernel, [PACKED], [WIDE, DENSE])(
        cotangent, state_one, *picks, over_exp(leaving)
    )
    grads_own, grads_mate = call(first_grad_kernel, [KEPT, KEPT], [WIDE, DENSE])(
        over_exp(leaving), wb, positive, gate
    )
    half, narrow = ((4 * SLOTS, D // 2), bf16), ((4 * SLOTS, G), bf16)
    chunk = (2 * G, LANE)
    near, far, next_chip, own_chip = call(
        weight_kernel,
        [((4, *chunk), bf16), ((1, *chunk), bf16), ((2, *chunk), f32), ((1, *chunk), f32)],
        [half, narrow, half, narrow],
    )(grads_own, both_cores(grads_mate), kept_own, kept_mate, one_own, one_mate)
    near, far = lax.ppermute(near, "ctx", around), lax.ppermute(far, "ctx", two_on)
    same, cross, give = call(relay_kernel, [(chunk, bf16)] * 3)(near, far, next_chip)
    same = lax.ppermute(same, "ctx", two_on)
    cross = lax.ppermute(cross, "ctx", [(a, b + 1 - 2 * (b % 2)) for a, b in two_on])
    grad_in, grad_out = call(total_kernel, [((1, LANE, G), f32), ((1, G, LANE), f32)])(
        own_chip, near, both_cores(give), same, cross
    )
    return (grad_in, grad_out)


def solution(mesh):
    placed = (
        P(("ctx", "exp"), None),
        P(("ctx", "exp"), None),
        P(None, ("ctx", "exp"), None),
        P("exp", "ctx", None),
        P("exp", None, "ctx"),
        P("ctx", "exp"),
    )
    return jax.shard_map(
        on_device,
        mesh=mesh,
        in_specs=placed,
        out_specs=(P("exp", "ctx", None), P("exp", None, "ctx")),
        check_vma=False,
    )
```

```python
import functools

import jax
import jax.numpy as jnp
from jax import lax
from jax.experimental import pallas as pl
from jax.experimental.pallas import tpu as pltpu
from jax.sharding import PartitionSpec as P

epsilon = 1e-06
TOK, D, G, EXPERTS, CAP = 128, 2048, 256, 32, 3
SLOTS = EXPERTS * CAP
LANE = 128
CHUNKS = D // LANE
PEER = CAP * CHUNKS
CHIPS = 8
SHARD = 2 * G + 16
bf16, f32 = jnp.bfloat16, jnp.float32


def iota(shape, dimension):
    return lax.broadcasted_iota(jnp.int32, shape, dimension)


def choose(ids):
    hit = iota((EXPERTS, TOK), 0) == ids
    earlier = jnp.where(iota((TOK, TOK), 0) < iota((TOK, TOK), 1), 1.0, 0.0).astype(bf16)
    before = jnp.dot(jnp.where(hit, 1.0, 0.0).astype(bf16), earlier, preferred_element_type=f32)
    position = jnp.sum(jnp.where(hit, before, 0.0), axis=0, keepdims=True).astype(jnp.int32)
    slot = jnp.where(position < CAP, ids * CAP + position, -1)
    return jnp.where(iota((SLOTS, TOK), 0) == slot, 1.0, 0.0).astype(bf16)


def to_slots(pick, rows):
    return jnp.dot(pick, rows, preferred_element_type=f32)


def to_tokens(pick, rows):
    return lax.dot_general(pick, rows, (((0,), (0,)), ((), ())), preferred_element_type=f32)


def pack(rows):
    return rows.astype(bf16).reshape(SLOTS, CHUNKS, LANE).reshape(SLOTS * CHUNKS, LANE)


def unpack(blocks):
    return blocks.reshape(SLOTS, CHUNKS, LANE).reshape(SLOTS, D)


def normalize(state):
    inverse = 1.0 / jnp.sqrt(jnp.mean(state * state, axis=-1, keepdims=True) + epsilon)
    return state * inverse, inverse


def share_kernel(weight_in, weight_out, router, out):
    out[:LANE, :] = weight_in[0, :, :LANE]
    out[LANE:G, :] = weight_in[0, :, LANE:]
    out[G : 2 * G, :] = weight_out[0]
    out[2 * G :, :] = jnp.broadcast_to(router[...], (SHARD - 2 * G, LANE))


def place(block, first, chip, wa, wb, column):
    for core in range(2):
        at = first + core * SHARD
        to = pl.ds(pl.multiple_of((2 * chip + core) * LANE, LANE), LANE)
        wa[to, :LANE] = block[at : at + LANE, :]
        wa[to, LANE:] = block[at + LANE : at + G, :]
        wb[:, to] = block[at + G : at + 2 * G, :]
        column[:, to] = block[at + 2 * G : at + 2 * G + 1, :].astype(f32)


def own_chunks(core):
    chip = lax.div(lax.axis_index("ctx"), 2)
    way = 1 - 2 * core

    def chunk(hops, parity):
        return 2 * lax.rem(chip + hops * way + CHIPS, CHIPS) + parity

    pairs = [chunk(hops, parity) for hops in (1, 3, 2) for parity in range(2)]
    return pairs[:4] + [chunk(4, core)] + pairs[4:] + [chunk(0, core)]


def split(full, narrow, own, mate, first=0):
    core = lax.rem(lax.axis_index("ctx"), 2)
    for half, chunks in ((own, own_chunks(core)), (mate, own_chunks(1 - core))):
        for i, chunk in enumerate(chunks):
            at = pl.ds(pl.multiple_of(chunk * LANE, LANE), LANE)
            half[:, first + i * LANE : first + (i + 1) * LANE] = full[:, at]
        half[:, first + D // 2 : first + HALF] = narrow


def forward(rows, wa, wb, column):
    before = jnp.dot(rows, wa[...], preferred_element_type=f32)
    positive = jnp.maximum(before, 0.0)
    hidden = (positive * positive).astype(bf16)
    expert_out = jnp.dot(hidden, wb[...], preferred_element_type=f32)
    logit = jnp.sum(rows.astype(f32) * column[...], axis=1, keepdims=True)
    gate = 1.0 / (1.0 + jnp.exp(-logit))
    return positive, hidden, expert_out, gate


def backward(upstream, wb, positive, gate):
    upper = upstream.astype(f32)
    grad_expert = (gate * upper).astype(bf16)
    grad_hidden = lax.dot_general(
        grad_expert, wb[...], (((1,), (1,)), ((), ())), preferred_element_type=f32
    )
    grad_pre = (grad_hidden * 2.0 * positive).astype(bf16)
    return upper, grad_expert, grad_pre


def dispatch_kernel(tokens, cotangent, ids, out, first, second, packed, sems):
    loads = []
    for i, (source, target) in enumerate(((tokens, first), (cotangent, second))):
        for j in range(4):
            rows = pl.ds(j * TOK // 4, TOK // 4)
            copy = pltpu.make_async_copy(source.at[rows, :], target.at[rows, :], sems.at[4 * i + j])
            copy.start()
            loads.append(copy)
    picks = choose(ids[0:1, :]), choose(ids[1:2, :])
    stores = []
    for i in range(2):
        for copy in loads[4 * i : 4 * i + 4]:
            copy.wait()
        rows = second[...] if i else normalize(first[...].astype(f32))[0].astype(bf16)
        packed[i] = pack(to_slots(picks[i], rows)).reshape(EXPERTS, PEER, LANE)
        copy = pltpu.make_async_copy(
            packed.at[i], out.at[:, pl.ds(i * PEER, PEER), :], sems.at[8 + i]
        )
        copy.start()
        stores.append(copy)
    for copy in stores:
        copy.wait()


def arrive_kernel(taken, rows, upstream):
    blocks = taken[...].reshape(EXPERTS, 2 * PEER, LANE)
    rows[...] = unpack(blocks[:, :PEER, :].reshape(EXPERTS * PEER, LANE))
    upstream[...] = unpack(blocks[:, PEER:, :].reshape(EXPERTS * PEER, LANE))


def first_kernel(
    rows, own, pair_1, pair_2, pair_3, far,
    out, positive_out, own_out, mate_out, gate_out, wa, wb, column
):
    chip = lax.div(lax.axis_index("ctx"), 2)
    place(own, 0, chip, wa, wb, column)
    for hop, pair in enumerate((pair_1, pair_2, pair_3), 1):
        place(pair, 0, lax.rem(chip + CHIPS - hop, CHIPS), wa, wb, column)
        place(pair, 2 * SHARD, lax.rem(chip + hop, CHIPS), wa, wb, column)
    place(far, 0, lax.rem(chip + CHIPS // 2, CHIPS), wa, wb, column)
    positive, hidden, expert_out, gate = forward(rows[...], wa, wb, column)
    out[...] = pack(gate * expert_out)
    positive_out[...] = positive
    split(rows, hidden, own_out, mate_out)
    gate_out[...] = jnp.broadcast_to(gate, (SLOTS, LANE))


def choose_kernel(ids, first, second):
    first[...] = choose(ids[0:1, :])
    second[...] = choose(ids[1:2, :])


def middle_kernel(tokens, pick_zero, pick_one, mixed, out, unit_out, inverse_out):
    state = tokens[...].astype(f32) + to_tokens(pick_zero[...], unpack(mixed[...]))
    unit, inverse = normalize(state)
    unit_out[...] = unit
    inverse_out[...] = jnp.broadcast_to(inverse, (TOK, LANE))
    out[...] = pack(to_slots(pick_one[...], unit.astype(bf16)))


def second_kernel(
    taken, upstream, wa, wb, column, out, rows, hidden_out, expert, pre
):
    rows[...] = unpack(taken[...])
    positive, hidden, expert_out, gate = forward(rows[...], wa, wb, column)
    upper, grad_expert, grad_pre = backward(upstream[...], wb, positive, gate)
    grad_gate = jnp.sum(upper * expert_out, axis=1, keepdims=True)
    grad_logit = grad_gate * gate * (1.0 - gate)
    flowing = lax.dot_general(
        grad_pre, wa[...], (((1,), (1,)), ((), ())), preferred_element_type=f32
    )
    out[...] = pack(flowing + grad_logit * column[...])
    hidden_out[...] = hidden
    expert[...] = grad_expert
    pre[...] = grad_pre


def split_kernel(rows, hidden, expert, pre, own, mate):
    split(rows, hidden[...], own, mate)
    split(expert, pre[...], own, mate, HALF)


def return_kernel(
    cotangent, unit_in, inverse, pick_zero, pick_one, taken, out
):
    unit = unit_in[...]
    grad = to_tokens(pick_one[...], unpack(taken[...]))
    inner = jnp.mean(grad * unit, axis=-1, keepdims=True)
    upstream = cotangent[...].astype(f32) + (grad - unit * inner) * inverse[:, :1]
    out[...] = pack(to_slots(pick_zero[...], upstream.astype(bf16)))


def over_rows(left, right):
    return lax.dot_general(left, right, (((0,), (0,)), ((), ())), preferred_element_type=f32)


def first_grad_kernel(taken, wb, positive, gate, own, mate, dense):
    _, grad_expert, grad_pre = backward(unpack(taken[...]), wb, positive[...], gate[:, :1])
    dense[...] = grad_expert
    split(dense, grad_pre, own, mate)


def weight_kernel(
    grads_own, grads_both, kept_own, kept_mate, one_own, one_mate,
    near, far, next_chip, own_chip, rows, hidden, grads, pre
):
    mate = pl.multiple_of((1 - lax.rem(lax.axis_index("ctx"), 2)) * SLOTS, SLOTS)
    kept = (kept_own[...], kept_mate[...], one_own[:, :HALF], one_mate[:, :HALF])
    grad = (grads_own[...], grads_both[pl.ds(mate, SLOTS), :], one_own[:, HALF:], one_mate[:, HALF:])
    for i in range(4):
        to = slice(i * SLOTS, (i + 1) * SLOTS)
        rows[to, :], hidden[to, :] = kept[i][:, : D // 2], kept[i][:, D // 2 :]
        grads[to, :], pre[to, :] = grad[i][:, : D // 2], grad[i][:, D // 2 :]
    part_in = over_rows(pre[...], rows[...])
    part_out = over_rows(hidden[...], grads[...])
    targets = [(near, i) for i in range(4)] + [(far, 0), (next_chip, 0), (next_chip, 1), (own_chip, 0)]
    for i, (out, to) in enumerate(targets):
        at = slice(i * LANE, (i + 1) * LANE)
        out[to, :G, :] = part_in[:, at].astype(out.dtype)
        out[to, G:, :] = part_out[:, at].astype(out.dtype)


def relay_kernel(near, far, next_chip, same, cross, give):
    core = lax.rem(lax.axis_index("ctx"), 2)
    same[...] = (
        next_chip[core] + near[2 + core].astype(f32) + far[0].astype(f32)
    ).astype(bf16)
    cross[...] = (next_chip[1 - core] + near[3 - core].astype(f32)).astype(bf16)
    give[...] = near[1 - core]


def total_kernel(own_chip, near, gives, same, cross, grad_in, grad_out):
    core = lax.rem(lax.axis_index("ctx"), 2)
    mate = pl.multiple_of((1 - core) * 2 * G, 2 * G)
    total = own_chip[0] + near[core].astype(f32) + gives[pl.ds(mate, 2 * G), :].astype(f32)
    total = total + same[...].astype(f32) + cross[...].astype(f32)
    grad_in[0] = total[:G, :].T
    grad_out[0] = total[G:, :]


def call(kernel, outs, scratch=(), room=24, cost=0):
    return pl.pallas_call(
        kernel,
        out_shape=[jax.ShapeDtypeStruct(s, t) for s, t in outs],
        scratch_shapes=[pltpu.VMEM(s, t) for s, t in scratch],
        compiler_params=pltpu.CompilerParams(vmem_limit_bytes=room << 20),
        cost_estimate=pl.CostEstimate(flops=cost, bytes_accessed=0, transcendentals=0)
        if cost
        else None,
    )


PACKED = ((EXPERTS * PEER, LANE), bf16)
DENSE = ((SLOTS, D), bf16)
PICK = ((SLOTS, TOK), bf16)
HALF = D // 2 + G
KEPT = ((SLOTS, HALF), bf16)
WEIGHTS = (((D, G), bf16), ((G, D), bf16), ((1, D), f32))


def over_exp(buffer):
    shaped = buffer.reshape(EXPERTS, -1, LANE)
    return lax.all_to_all(shaped, "exp", 0, 0, tiled=True).reshape(buffer.shape)


def on_device(tokens, cotangent, expert_ids, weight_in, weight_out, router):
    chips = lax.axis_size("ctx") // 2
    ids = expert_ids[:, :, 0]
    cores = [[2 * z, 2 * z + 1] for z in range(chips)]

    def both_cores(value):
        return lax.all_gather(value, "ctx", axis=0, tiled=True, axis_index_groups=cores)

    around = [(2 * z, 2 * ((z + 1) % chips)) for z in range(chips)]
    around += [(2 * z + 1, 2 * ((z - 1) % chips) + 1) for z in range(chips)]
    (share,) = call(share_kernel, [((SHARD, LANE), bf16)], room=60)(
        weight_in, weight_out, router.reshape(1, LANE)
    )
    own = both_cores(share)
    far_away = pl.BlockSpec(memory_space=pl.ANY)
    leaving = pl.pallas_call(
        dispatch_kernel,
        out_shape=jax.ShapeDtypeStruct((EXPERTS, 2 * PEER, LANE), bf16),
        in_specs=[far_away, far_away, pl.BlockSpec(memory_space=pltpu.VMEM)],
        out_specs=far_away,
        scratch_shapes=[
            pltpu.VMEM((TOK, D), bf16),
            pltpu.VMEM((TOK, D), bf16),
            pltpu.VMEM((2, EXPERTS, PEER, LANE), bf16),
            pltpu.SemaphoreType.DMA((10,)),
        ],
        compiler_params=pltpu.CompilerParams(vmem_limit_bytes=60 << 20),
    )(tokens, cotangent, ids).reshape(2 * EXPERTS * PEER, LANE)
    two_on = [
        (2 * z + c, 2 * ((z + 2 - 4 * c) % chips) + c) for z in range(chips) for c in range(2)
    ]
    two = lax.ppermute(own, "ctx", two_on)
    later, two = lax.optimization_barrier((own, two))
    _, two = lax.optimization_barrier((leaving, two))
    one = lax.ppermute(later, "ctx", around)
    three, four = lax.ppermute(two, "ctx", around), lax.ppermute(two, "ctx", two_on)
    pairs = [both_cores(one), both_cores(two)]
    ids, *pairs = lax.optimization_barrier((ids, *pairs))
    picks = call(choose_kernel, [PICK, PICK], cost=8 * 1150000000)(ids)
    three, *picks = lax.optimization_barrier((three, *picks))
    pairs += [both_cores(three), four]
    rows_zero, upstream_one = call(arrive_kernel, [DENSE, DENSE])(over_exp(leaving))
    mixed, positive, kept_own, kept_mate, gate, wa, wb, column = call(
        first_kernel,
        [PACKED, ((SLOTS, G), f32), KEPT, KEPT, ((SLOTS, LANE), f32), *WEIGHTS],
    )(rows_zero, own, *pairs)
    across = [(2 * z + c, 2 * z + 1 - c) for z in range(chips) for c in range(2)]
    kept_mate = lax.ppermute(kept_mate, "ctx", across)
    leaving, *unit_one = call(
        middle_kernel, [PACKED, ((TOK, D), f32), ((TOK, LANE), f32)]
    )(
        tokens, *picks, over_exp(mixed)
    )
    double = ((SLOTS, 2 * HALF), bf16)
    slim = ((SLOTS, G), bf16)
    leaving, *second = call(second_kernel, [PACKED, DENSE, slim, DENSE, slim])(
        over_exp(leaving), upstream_one, wa, wb, column
    )
    one_own, one_mate = call(split_kernel, [double, double])(*second)
    one_mate = lax.ppermute(one_mate, "ctx", across)
    (leaving,) = call(return_kernel, [PACKED])(
        cotangent, *unit_one, *picks, over_exp(leaving)
    )
    grads_own, grads_mate = call(first_grad_kernel, [KEPT, KEPT], [DENSE])(
        over_exp(leaving), wb, positive, gate
    )
    half, narrow = ((4 * SLOTS, D // 2), bf16), ((4 * SLOTS, G), bf16)
    chunk = (2 * G, LANE)
    near, far, next_chip, own_chip = call(
        weight_kernel,
        [((4, *chunk), bf16), ((1, *chunk), bf16), ((2, *chunk), f32), ((1, *chunk), f32)],
        [half, narrow, half, narrow],
    )(grads_own, both_cores(grads_mate), kept_own, kept_mate, one_own, one_mate)
    near, far = lax.ppermute(near, "ctx", around), lax.ppermute(far, "ctx", two_on)
    same, cross, give = call(relay_kernel, [(chunk, bf16)] * 3)(near, far, next_chip)
    same = lax.ppermute(same, "ctx", two_on)
    cross = lax.ppermute(cross, "ctx", [(a, b + 1 - 2 * (b % 2)) for a, b in two_on])
    grad_in, grad_out = call(total_kernel, [((1, LANE, G), f32), ((1, G, LANE), f32)])(
        own_chip, near, both_cores(give), same, cross
    )
    return (grad_in, grad_out)


def solution(mesh):
    placed = (
        P(("ctx", "exp"), None),
        P(("ctx", "exp"), None),
        P(None, ("ctx", "exp"), None),
        P("exp", "ctx", None),
        P("exp", None, "ctx"),
        P("ctx", "exp"),
    )
    return jax.shard_map(
        on_device,
        mesh=mesh,
        in_specs=placed,
        out_specs=(P("exp", "ctx", None), P("exp", None, "ctx")),
        check_vma=False,
    )
```

```python
import functools

import jax
import jax.numpy as jnp
from jax import lax
from jax.experimental import pallas as pl
from jax.experimental.pallas import tpu as pltpu
from jax.sharding import PartitionSpec as P

epsilon = 1e-06
TOK, D, G, EXPERTS, CAP = 128, 2048, 256, 32, 3
SLOTS = EXPERTS * CAP
LANE = 128
CHUNKS = D // LANE
PEER = CAP * CHUNKS
CHIPS = 8
SHARD = 2 * G + 16
bf16, f32 = jnp.bfloat16, jnp.float32


def iota(shape, dimension):
    return lax.broadcasted_iota(jnp.int32, shape, dimension)


def choose(ids):
    hit = iota((EXPERTS, TOK), 0) == ids
    earlier = jnp.where(iota((TOK, TOK), 0) < iota((TOK, TOK), 1), 1.0, 0.0).astype(bf16)
    before = jnp.dot(jnp.where(hit, 1.0, 0.0).astype(bf16), earlier, preferred_element_type=f32)
    position = jnp.sum(jnp.where(hit, before, 0.0), axis=0, keepdims=True).astype(jnp.int32)
    slot = jnp.where(position < CAP, ids * CAP + position, -1)
    return jnp.where(iota((SLOTS, TOK), 0) == slot, 1.0, 0.0).astype(bf16)


def to_slots(pick, rows):
    return jnp.dot(pick, rows, preferred_element_type=f32)


def to_tokens(pick, rows):
    return lax.dot_general(pick, rows, (((0,), (0,)), ((), ())), preferred_element_type=f32)


def pack(rows):
    return rows.astype(bf16).reshape(SLOTS, CHUNKS, LANE).reshape(SLOTS * CHUNKS, LANE)


def unpack(blocks):
    return blocks.reshape(SLOTS, CHUNKS, LANE).reshape(SLOTS, D)


def normalize(state):
    inverse = 1.0 / jnp.sqrt(jnp.mean(state * state, axis=-1, keepdims=True) + epsilon)
    return state * inverse, inverse


def share_kernel(weight_in, weight_out, router, out):
    out[:LANE, :] = weight_in[0, :, :LANE]
    out[LANE:G, :] = weight_in[0, :, LANE:]
    out[G : 2 * G, :] = weight_out[0]
    out[2 * G :, :] = jnp.broadcast_to(router[...], (SHARD - 2 * G, LANE))


def place(block, first, chip, wa, wb, column):
    for core in range(2):
        at = first + core * SHARD
        to = pl.ds(pl.multiple_of((2 * chip + core) * LANE, LANE), LANE)
        wa[to, :LANE] = block[at : at + LANE, :]
        wa[to, LANE:] = block[at + LANE : at + G, :]
        wb[:, to] = block[at + G : at + 2 * G, :]
        column[:, to] = block[at + 2 * G : at + 2 * G + 1, :].astype(f32)


def own_chunks(core):
    chip = lax.div(lax.axis_index("ctx"), 2)
    way = 1 - 2 * core

    def chunk(hops, parity):
        return 2 * lax.rem(chip + hops * way + CHIPS, CHIPS) + parity

    pairs = [chunk(hops, parity) for hops in (1, 3, 2) for parity in range(2)]
    return pairs[:4] + [chunk(4, core)] + pairs[4:] + [chunk(0, core)]


def split(full, narrow, own, mate, first=0):
    core = lax.rem(lax.axis_index("ctx"), 2)
    for half, chunks in ((own, own_chunks(core)), (mate, own_chunks(1 - core))):
        for i, chunk in enumerate(chunks):
            at = pl.ds(pl.multiple_of(chunk * LANE, LANE), LANE)
            half[:, first + i * LANE : first + (i + 1) * LANE] = full[:, at]
        half[:, first + D // 2 : first + HALF] = narrow


def forward(rows, wa, wb, column):
    before = jnp.dot(rows, wa[...], preferred_element_type=f32)
    positive = jnp.maximum(before, 0.0)
    hidden = (positive * positive).astype(bf16)
    expert_out = jnp.dot(hidden, wb[...], preferred_element_type=f32)
    logit = jnp.sum(rows.astype(f32) * column[...], axis=1, keepdims=True)
    gate = 1.0 / (1.0 + jnp.exp(-logit))
    return positive, hidden, expert_out, gate


def backward(upstream, wb, positive, gate):
    upper = upstream.astype(f32)
    grad_expert = (gate * upper).astype(bf16)
    grad_hidden = lax.dot_general(
        grad_expert, wb[...], (((1,), (1,)), ((), ())), preferred_element_type=f32
    )
    grad_pre = (grad_hidden * 2.0 * positive).astype(bf16)
    return upper, grad_expert, grad_pre


def dispatch_kernel(tokens, cotangent, ids, out):
    unit, _ = normalize(tokens[...].astype(f32))
    rows = to_slots(choose(ids[0:1, :]), unit.astype(bf16))
    out[:, :PEER, :] = pack(rows).reshape(EXPERTS, PEER, LANE)
    rows = to_slots(choose(ids[1:2, :]), cotangent[...])
    out[:, PEER:, :] = pack(rows).reshape(EXPERTS, PEER, LANE)


def arrive_kernel(taken, rows, upstream):
    blocks = taken[...].reshape(EXPERTS, 2 * PEER, LANE)
    rows[...] = unpack(blocks[:, :PEER, :].reshape(EXPERTS * PEER, LANE))
    upstream[...] = unpack(blocks[:, PEER:, :].reshape(EXPERTS * PEER, LANE))


def first_kernel(
    rows, own, pair_1, pair_2, pair_3, far,
    out, positive_out, own_out, mate_out, gate_out, wa, wb, column
):
    chip = lax.div(lax.axis_index("ctx"), 2)
    place(own, 0, chip, wa, wb, column)
    for hop, pair in enumerate((pair_1, pair_2, pair_3), 1):
        place(pair, 0, lax.rem(chip + CHIPS - hop, CHIPS), wa, wb, column)
        place(pair, 2 * SHARD, lax.rem(chip + hop, CHIPS), wa, wb, column)
    place(far, 0, lax.rem(chip + CHIPS // 2, CHIPS), wa, wb, column)
    positive, hidden, expert_out, gate = forward(rows[...], wa, wb, column)
    out[...] = pack(gate * expert_out)
    positive_out[...] = positive
    split(rows, hidden, own_out, mate_out)
    gate_out[...] = jnp.broadcast_to(gate, (SLOTS, LANE))


def choose_kernel(ids, first, second):
    first[...] = choose(ids[0:1, :])
    second[...] = choose(ids[1:2, :])


def middle_kernel(tokens, pick_zero, pick_one, mixed, out, unit_out, inverse_out):
    state = tokens[...].astype(f32) + to_tokens(pick_zero[...], unpack(mixed[...]))
    unit, inverse = normalize(state)
    unit_out[...] = unit
    inverse_out[...] = jnp.broadcast_to(inverse, (TOK, LANE))
    out[...] = pack(to_slots(pick_one[...], unit.astype(bf16)))


def second_kernel(
    taken, upstream, wa, wb, column, out, rows, hidden_out, expert, pre
):
    rows[...] = unpack(taken[...])
    positive, hidden, expert_out, gate = forward(rows[...], wa, wb, column)
    upper, grad_expert, grad_pre = backward(upstream[...], wb, positive, gate)
    grad_gate = jnp.sum(upper * expert_out, axis=1, keepdims=True)
    grad_logit = grad_gate * gate * (1.0 - gate)
    flowing = lax.dot_general(
        grad_pre, wa[...], (((1,), (1,)), ((), ())), preferred_element_type=f32
    )
    out[...] = pack(flowing + grad_logit * column[...])
    hidden_out[...] = hidden
    expert[...] = grad_expert
    pre[...] = grad_pre


def split_kernel(rows, hidden, expert, pre, own, mate):
    split(rows, hidden[...], own, mate)
    split(expert, pre[...], own, mate, HALF)


def return_kernel(
    cotangent, unit_in, inverse, pick_zero, pick_one, taken, out
):
    unit = unit_in[...]
    grad = to_tokens(pick_one[...], unpack(taken[...]))
    inner = jnp.mean(grad * unit, axis=-1, keepdims=True)
    upstream = cotangent[...].astype(f32) + (grad - unit * inner) * inverse[:, :1]
    out[...] = pack(to_slots(pick_zero[...], upstream.astype(bf16)))


def over_rows(left, right):
    return lax.dot_general(left, right, (((0,), (0,)), ((), ())), preferred_element_type=f32)


def first_grad_kernel(taken, wb, positive, gate, own, mate, dense):
    _, grad_expert, grad_pre = backward(unpack(taken[...]), wb, positive[...], gate[:, :1])
    dense[...] = grad_expert
    split(dense, grad_pre, own, mate)


def weight_kernel(
    grads_own, grads_both, kept_own, kept_mate, one_own, one_mate,
    near, far, next_chip, own_chip, rows, hidden, grads, pre
):
    mate = pl.multiple_of((1 - lax.rem(lax.axis_index("ctx"), 2)) * SLOTS, SLOTS)
    kept = (kept_own[...], kept_mate[...], one_own[:, :HALF], one_mate[:, :HALF])
    grad = (grads_own[...], grads_both[pl.ds(mate, SLOTS), :], one_own[:, HALF:], one_mate[:, HALF:])
    for i in range(4):
        to = slice(i * SLOTS, (i + 1) * SLOTS)
        rows[to, :], hidden[to, :] = kept[i][:, : D // 2], kept[i][:, D // 2 :]
        grads[to, :], pre[to, :] = grad[i][:, : D // 2], grad[i][:, D // 2 :]
    part_in = over_rows(pre[...], rows[...])
    part_out = over_rows(hidden[...], grads[...])
    targets = [(near, i) for i in range(4)] + [(far, 0), (next_chip, 0), (next_chip, 1), (own_chip, 0)]
    for i, (out, to) in enumerate(targets):
        at = slice(i * LANE, (i + 1) * LANE)
        out[to, :G, :] = part_in[:, at].astype(out.dtype)
        out[to, G:, :] = part_out[:, at].astype(out.dtype)


def relay_kernel(near, far, next_chip, same, cross, give):
    core = lax.rem(lax.axis_index("ctx"), 2)
    same[...] = (
        next_chip[core] + near[2 + core].astype(f32) + far[0].astype(f32)
    ).astype(bf16)
    cross[...] = (next_chip[1 - core] + near[3 - core].astype(f32)).astype(bf16)
    give[...] = near[1 - core]


def total_kernel(own_chip, near, gives, same, cross, grad_in, grad_out):
    core = lax.rem(lax.axis_index("ctx"), 2)
    mate = pl.multiple_of((1 - core) * 2 * G, 2 * G)
    total = own_chip[0] + near[core].astype(f32) + gives[pl.ds(mate, 2 * G), :].astype(f32)
    total = total + same[...].astype(f32) + cross[...].astype(f32)
    grad_in[0] = total[:G, :].T
    grad_out[0] = total[G:, :]


def call(kernel, outs, scratch=(), room=24, cost=0):
    return pl.pallas_call(
        kernel,
        out_shape=[jax.ShapeDtypeStruct(s, t) for s, t in outs],
        scratch_shapes=[pltpu.VMEM(s, t) for s, t in scratch],
        compiler_params=pltpu.CompilerParams(vmem_limit_bytes=room << 20),
        cost_estimate=pl.CostEstimate(flops=cost, bytes_accessed=0, transcendentals=0)
        if cost
        else None,
    )


PACKED = ((EXPERTS * PEER, LANE), bf16)
DENSE = ((SLOTS, D), bf16)
PICK = ((SLOTS, TOK), bf16)
HALF = D // 2 + G
KEPT = ((SLOTS, HALF), bf16)
WEIGHTS = (((D, G), bf16), ((G, D), bf16), ((1, D), f32))


def over_exp(buffer):
    shaped = buffer.reshape(EXPERTS, -1, LANE)
    return lax.all_to_all(shaped, "exp", 0, 0, tiled=True).reshape(buffer.shape)


def on_device(tokens, cotangent, expert_ids, weight_in, weight_out, router):
    chips = lax.axis_size("ctx") // 2
    ids = expert_ids[:, :, 0]
    cores = [[2 * z, 2 * z + 1] for z in range(chips)]

    def both_cores(value):
        return lax.all_gather(value, "ctx", axis=0, tiled=True, axis_index_groups=cores)

    around = [(2 * z, 2 * ((z + 1) % chips)) for z in range(chips)]
    around += [(2 * z + 1, 2 * ((z - 1) % chips) + 1) for z in range(chips)]
    (share,) = call(share_kernel, [((SHARD, LANE), bf16)], room=60)(
        weight_in, weight_out, router.reshape(1, LANE)
    )
    own = both_cores(share)
    (leaving,) = call(dispatch_kernel, [((EXPERTS, 2 * PEER, LANE), bf16)], room=60)(
        tokens, cotangent, ids
    )
    leaving = leaving.reshape(2 * EXPERTS * PEER, LANE)
    two_on = [
        (2 * z + c, 2 * ((z + 2 - 4 * c) % chips) + c) for z in range(chips) for c in range(2)
    ]
    two = lax.ppermute(own, "ctx", two_on)
    later, two = lax.optimization_barrier((own, two))
    _, two = lax.optimization_barrier((leaving, two))
    one = lax.ppermute(later, "ctx", around)
    three, four = lax.ppermute(two, "ctx", around), lax.ppermute(two, "ctx", two_on)
    pairs = [both_cores(one), both_cores(two)]
    ids, *pairs = lax.optimization_barrier((ids, *pairs))
    picks = call(choose_kernel, [PICK, PICK], cost=8 * 1150000000)(ids)
    three, *picks = lax.optimization_barrier((three, *picks))
    pairs += [both_cores(three), four]
    rows_zero, upstream_one = call(arrive_kernel, [DENSE, DENSE])(over_exp(leaving))
    mixed, positive, kept_own, kept_mate, gate, wa, wb, column = call(
        first_kernel,
        [PACKED, ((SLOTS, G), f32), KEPT, KEPT, ((SLOTS, LANE), f32), *WEIGHTS],
    )(rows_zero, own, *pairs)
    across = [(2 * z + c, 2 * z + 1 - c) for z in range(chips) for c in range(2)]
    kept_mate = lax.ppermute(kept_mate, "ctx", across)
    leaving, *unit_one = call(
        middle_kernel, [PACKED, ((TOK, D), f32), ((TOK, LANE), f32)]
    )(
        tokens, *picks, over_exp(mixed)
    )
    double = ((SLOTS, 2 * HALF), bf16)
    slim = ((SLOTS, G), bf16)
    leaving, *second = call(second_kernel, [PACKED, DENSE, slim, DENSE, slim])(
        over_exp(leaving), upstream_one, wa, wb, column
    )
    one_own, one_mate = call(split_kernel, [double, double])(*second)
    one_mate = lax.ppermute(one_mate, "ctx", across)
    (leaving,) = call(return_kernel, [PACKED])(
        cotangent, *unit_one, *picks, over_exp(leaving)
    )
    grads_own, grads_mate = call(first_grad_kernel, [KEPT, KEPT], [DENSE])(
        over_exp(leaving), wb, positive, gate
    )
    half, narrow = ((4 * SLOTS, D // 2), bf16), ((4 * SLOTS, G), bf16)
    chunk = (2 * G, LANE)
    near, far, next_chip, own_chip = call(
        weight_kernel,
        [((4, *chunk), bf16), ((1, *chunk), bf16), ((2, *chunk), f32), ((1, *chunk), f32)],
        [half, narrow, half, narrow],
    )(grads_own, both_cores(grads_mate), kept_own, kept_mate, one_own, one_mate)
    near, far = lax.ppermute(near, "ctx", around), lax.ppermute(far, "ctx", two_on)
    same, cross, give = call(relay_kernel, [(chunk, bf16)] * 3)(near, far, next_chip)
    same = lax.ppermute(same, "ctx", two_on)
    cross = lax.ppermute(cross, "ctx", [(a, b + 1 - 2 * (b % 2)) for a, b in two_on])
    grad_in, grad_out = call(total_kernel, [((1, LANE, G), f32), ((1, G, LANE), f32)])(
        own_chip, near, both_cores(give), same, cross
    )
    return (grad_in, grad_out)


def solution(mesh):
    placed = (
        P(("ctx", "exp"), None),
        P(("ctx", "exp"), None),
        P(None, ("ctx", "exp"), None),
        P("exp", "ctx", None),
        P("exp", None, "ctx"),
        P("ctx", "exp"),
    )
    return jax.shard_map(
        on_device,
        mesh=mesh,
        in_specs=placed,
        out_specs=(P("exp", "ctx", None), P("exp", None, "ctx")),
        check_vma=False,
    )
```

```python
import functools

import jax
import jax.numpy as jnp
from jax import lax
from jax.experimental import pallas as pl
from jax.experimental.pallas import tpu as pltpu
from jax.sharding import PartitionSpec as P

epsilon = 1e-06
TOK, D, G, EXPERTS, CAP = 128, 2048, 256, 32, 3
SLOTS = EXPERTS * CAP
LANE = 128
CHUNKS = D // LANE
PEER = CAP * CHUNKS
CHIPS = 8
SHARD = 2 * G + 16
bf16, f32 = jnp.bfloat16, jnp.float32


def iota(shape, dimension):
    return lax.broadcasted_iota(jnp.int32, shape, dimension)


def choose(ids):
    hit = iota((EXPERTS, TOK), 0) == ids
    earlier = jnp.where(iota((TOK, TOK), 0) < iota((TOK, TOK), 1), 1.0, 0.0).astype(bf16)
    before = jnp.dot(jnp.where(hit, 1.0, 0.0).astype(bf16), earlier, preferred_element_type=f32)
    position = jnp.sum(jnp.where(hit, before, 0.0), axis=0, keepdims=True).astype(jnp.int32)
    slot = jnp.where(position < CAP, ids * CAP + position, -1)
    return jnp.where(iota((SLOTS, TOK), 0) == slot, 1.0, 0.0).astype(bf16)


def to_slots(pick, rows):
    return jnp.dot(pick, rows, preferred_element_type=f32)


def to_tokens(pick, rows):
    return lax.dot_general(pick, rows, (((0,), (0,)), ((), ())), preferred_element_type=f32)


def pack(rows):
    return rows.astype(bf16).reshape(SLOTS, CHUNKS, LANE).reshape(SLOTS * CHUNKS, LANE)


def unpack(blocks):
    return blocks.reshape(SLOTS, CHUNKS, LANE).reshape(SLOTS, D)


def normalize(state):
    inverse = 1.0 / jnp.sqrt(jnp.mean(state * state, axis=-1, keepdims=True) + epsilon)
    return state * inverse, inverse


def share_kernel(weight_in, weight_out, router, out):
    out[:LANE, :] = weight_in[0, :, :LANE]
    out[LANE:G, :] = weight_in[0, :, LANE:]
    out[G : 2 * G, :] = weight_out[0]
    out[2 * G :, :] = jnp.broadcast_to(router[...], (SHARD - 2 * G, LANE))


def place(block, first, chip, wa, wb, column):
    for core in range(2):
        at = first + core * SHARD
        to = pl.ds(pl.multiple_of((2 * chip + core) * LANE, LANE), LANE)
        wa[to, :LANE] = block[at : at + LANE, :]
        wa[to, LANE:] = block[at + LANE : at + G, :]
        wb[:, to] = block[at + G : at + 2 * G, :]
        column[:, to] = block[at + 2 * G : at + 2 * G + 1, :].astype(f32)


def own_chunks(core):
    chip = lax.div(lax.axis_index("ctx"), 2)
    way = 1 - 2 * core

    def chunk(hops, parity):
        return 2 * lax.rem(chip + hops * way + CHIPS, CHIPS) + parity

    pairs = [chunk(hops, parity) for hops in (1, 3, 2) for parity in range(2)]
    return pairs[:4] + [chunk(4, core)] + pairs[4:] + [chunk(0, core)]


def split(full, narrow, own, mate, first=0):
    core = lax.rem(lax.axis_index("ctx"), 2)
    for half, chunks in ((own, own_chunks(core)), (mate, own_chunks(1 - core))):
        for i, chunk in enumerate(chunks):
            at = pl.ds(pl.multiple_of(chunk * LANE, LANE), LANE)
            half[:, first + i * LANE : first + (i + 1) * LANE] = full[:, at]
        half[:, first + D // 2 : first + HALF] = narrow


def forward(rows, wa, wb, column):
    before = jnp.dot(rows, wa[...], preferred_element_type=f32)
    positive = jnp.maximum(before, 0.0)
    hidden = (positive * positive).astype(bf16)
    expert_out = jnp.dot(hidden, wb[...], preferred_element_type=f32)
    logit = jnp.sum(rows.astype(f32) * column[...], axis=1, keepdims=True)
    gate = 1.0 / (1.0 + jnp.exp(-logit))
    return positive, hidden, expert_out, gate


def backward(upstream, wb, positive, gate):
    upper = upstream.astype(f32)
    grad_expert = (gate * upper).astype(bf16)
    grad_hidden = lax.dot_general(
        grad_expert, wb[...], (((1,), (1,)), ((), ())), preferred_element_type=f32
    )
    grad_pre = (grad_hidden * 2.0 * positive).astype(bf16)
    return upper, grad_expert, grad_pre


def dispatch_kernel(tokens, cotangent, ids, out):
    unit, _ = normalize(tokens[...].astype(f32))
    rows = to_slots(choose(ids[0:1, :]), unit.astype(bf16))
    out[:, :PEER, :] = pack(rows).reshape(EXPERTS, PEER, LANE)
    rows = to_slots(choose(ids[1:2, :]), cotangent[...])
    out[:, PEER:, :] = pack(rows).reshape(EXPERTS, PEER, LANE)


def arrive_kernel(taken, rows, upstream):
    blocks = taken[...].reshape(EXPERTS, 2 * PEER, LANE)
    rows[...] = unpack(blocks[:, :PEER, :].reshape(EXPERTS * PEER, LANE))
    upstream[...] = unpack(blocks[:, PEER:, :].reshape(EXPERTS * PEER, LANE))


def first_kernel(
    rows, own, pair_1, pair_2, pair_3, far,
    out, positive_out, own_out, mate_out, gate_out, wa, wb, column
):
    chip = lax.div(lax.axis_index("ctx"), 2)
    place(own, 0, chip, wa, wb, column)
    for hop, pair in enumerate((pair_1, pair_2, pair_3), 1):
        place(pair, 0, lax.rem(chip + CHIPS - hop, CHIPS), wa, wb, column)
        place(pair, 2 * SHARD, lax.rem(chip + hop, CHIPS), wa, wb, column)
    place(far, 0, lax.rem(chip + CHIPS // 2, CHIPS), wa, wb, column)
    positive, hidden, expert_out, gate = forward(rows[...], wa, wb, column)
    out[...] = pack(gate * expert_out)
    positive_out[...] = positive
    split(rows, hidden, own_out, mate_out)
    gate_out[...] = jnp.broadcast_to(gate, (SLOTS, LANE))


def choose_kernel(ids, first, second):
    first[...] = choose(ids[0:1, :])
    second[...] = choose(ids[1:2, :])


def middle_kernel(tokens, pick_zero, pick_one, mixed, out, unit_out, inverse_out):
    state = tokens[...].astype(f32) + to_tokens(pick_zero[...], unpack(mixed[...]))
    unit, inverse = normalize(state)
    unit_out[...] = unit
    inverse_out[...] = jnp.broadcast_to(inverse, (TOK, LANE))
    out[...] = pack(to_slots(pick_one[...], unit.astype(bf16)))


def second_kernel(
    taken, upstream, wa, wb, column, out, rows, hidden_out, expert, pre
):
    rows[...] = unpack(taken[...])
    positive, hidden, expert_out, gate = forward(rows[...], wa, wb, column)
    upper, grad_expert, grad_pre = backward(upstream[...], wb, positive, gate)
    grad_gate = jnp.sum(upper * expert_out, axis=1, keepdims=True)
    grad_logit = grad_gate * gate * (1.0 - gate)
    flowing = lax.dot_general(
        grad_pre, wa[...], (((1,), (1,)), ((), ())), preferred_element_type=f32
    )
    out[...] = pack(flowing + grad_logit * column[...])
    hidden_out[...] = hidden
    expert[...] = grad_expert
    pre[...] = grad_pre


def split_kernel(rows, hidden, expert, pre, own, mate):
    split(rows, hidden[...], own, mate)
    split(expert, pre[...], own, mate, HALF)


def return_kernel(
    cotangent, unit_in, inverse, pick_zero, pick_one, taken, out
):
    unit = unit_in[...]
    grad = to_tokens(pick_one[...], unpack(taken[...]))
    inner = jnp.mean(grad * unit, axis=-1, keepdims=True)
    upstream = cotangent[...].astype(f32) + (grad - unit * inner) * inverse[:, :1]
    out[...] = pack(to_slots(pick_zero[...], upstream.astype(bf16)))


def over_rows(left, right):
    return lax.dot_general(left, right, (((0,), (0,)), ((), ())), preferred_element_type=f32)


def first_grad_kernel(taken, wb, positive, gate, own, mate, dense):
    _, grad_expert, grad_pre = backward(unpack(taken[...]), wb, positive[...], gate[:, :1])
    dense[...] = grad_expert
    split(dense, grad_pre, own, mate)


def weight_kernel(
    grads_own, grads_both, kept_own, kept_mate, one_own, one_mate,
    near, far, next_chip, own_chip, rows, hidden, grads, pre
):
    mate = pl.multiple_of((1 - lax.rem(lax.axis_index("ctx"), 2)) * SLOTS, SLOTS)
    kept = (kept_own[...], kept_mate[...], one_own[:, :HALF], one_mate[:, :HALF])
    grad = (grads_own[...], grads_both[pl.ds(mate, SLOTS), :], one_own[:, HALF:], one_mate[:, HALF:])
    for i in range(4):
        to = slice(i * SLOTS, (i + 1) * SLOTS)
        rows[to, :], hidden[to, :] = kept[i][:, : D // 2], kept[i][:, D // 2 :]
        grads[to, :], pre[to, :] = grad[i][:, : D // 2], grad[i][:, D // 2 :]
    part_in = over_rows(pre[...], rows[...])
    part_out = over_rows(hidden[...], grads[...])
    targets = [(near, i) for i in range(4)] + [(far, 0), (next_chip, 0), (next_chip, 1), (own_chip, 0)]
    for i, (out, to) in enumerate(targets):
        at = slice(i * LANE, (i + 1) * LANE)
        out[to, :G, :] = part_in[:, at].astype(out.dtype)
        out[to, G:, :] = part_out[:, at].astype(out.dtype)


def cross_kernel(near, next_chip, cross, give):
    core = lax.rem(lax.axis_index("ctx"), 2)
    cross[...] = (next_chip[1 - core] + near[3 - core].astype(f32)).astype(bf16)
    give[...] = near[1 - core]


def same_kernel(near, far, next_chip, same):
    core = lax.rem(lax.axis_index("ctx"), 2)
    same[...] = (
        next_chip[core] + near[2 + core].astype(f32) + far[0].astype(f32)
    ).astype(bf16)


def total_kernel(own_chip, near, gives, same, cross, grad_in, grad_out):
    core = lax.rem(lax.axis_index("ctx"), 2)
    mate = pl.multiple_of((1 - core) * 2 * G, 2 * G)
    total = own_chip[0] + near[core].astype(f32) + gives[pl.ds(mate, 2 * G), :].astype(f32)
    total = total + same[...].astype(f32) + cross[...].astype(f32)
    grad_in[0] = total[:G, :].T
    grad_out[0] = total[G:, :]


def call(kernel, outs, scratch=(), room=24, cost=0):
    return pl.pallas_call(
        kernel,
        out_shape=[jax.ShapeDtypeStruct(s, t) for s, t in outs],
        scratch_shapes=[pltpu.VMEM(s, t) for s, t in scratch],
        compiler_params=pltpu.CompilerParams(vmem_limit_bytes=room << 20),
        cost_estimate=pl.CostEstimate(flops=cost, bytes_accessed=0, transcendentals=0)
        if cost
        else None,
    )


PACKED = ((EXPERTS * PEER, LANE), bf16)
DENSE = ((SLOTS, D), bf16)
PICK = ((SLOTS, TOK), bf16)
HALF = D // 2 + G
KEPT = ((SLOTS, HALF), bf16)
WEIGHTS = (((D, G), bf16), ((G, D), bf16), ((1, D), f32))


def over_exp(buffer):
    shaped = buffer.reshape(EXPERTS, -1, LANE)
    return lax.all_to_all(shaped, "exp", 0, 0, tiled=True).reshape(buffer.shape)


def on_device(tokens, cotangent, expert_ids, weight_in, weight_out, router):
    chips = lax.axis_size("ctx") // 2
    ids = expert_ids[:, :, 0]
    cores = [[2 * z, 2 * z + 1] for z in range(chips)]

    def both_cores(value):
        return lax.all_gather(value, "ctx", axis=0, tiled=True, axis_index_groups=cores)

    around = [(2 * z, 2 * ((z + 1) % chips)) for z in range(chips)]
    around += [(2 * z + 1, 2 * ((z - 1) % chips) + 1) for z in range(chips)]
    (share,) = call(share_kernel, [((SHARD, LANE), bf16)], room=60)(
        weight_in, weight_out, router.reshape(1, LANE)
    )
    own = both_cores(share)
    (leaving,) = call(dispatch_kernel, [((EXPERTS, 2 * PEER, LANE), bf16)], room=60)(
        tokens, cotangent, ids
    )
    leaving = leaving.reshape(2 * EXPERTS * PEER, LANE)
    two_on = [
        (2 * z + c, 2 * ((z + 2 - 4 * c) % chips) + c) for z in range(chips) for c in range(2)
    ]
    two = lax.ppermute(own, "ctx", two_on)
    later, two = lax.optimization_barrier((own, two))
    _, two = lax.optimization_barrier((leaving, two))
    one = lax.ppermute(later, "ctx", around)
    three, four = lax.ppermute(two, "ctx", around), lax.ppermute(two, "ctx", two_on)
    pairs = [both_cores(one), both_cores(two)]
    ids, *pairs = lax.optimization_barrier((ids, *pairs))
    picks = call(choose_kernel, [PICK, PICK], cost=8 * 1150000000)(ids)
    three, *picks = lax.optimization_barrier((three, *picks))
    pairs += [both_cores(three), four]
    rows_zero, upstream_one = call(arrive_kernel, [DENSE, DENSE])(over_exp(leaving))
    mixed, positive, kept_own, kept_mate, gate, wa, wb, column = call(
        first_kernel,
        [PACKED, ((SLOTS, G), f32), KEPT, KEPT, ((SLOTS, LANE), f32), *WEIGHTS],
    )(rows_zero, own, *pairs)
    across = [(2 * z + c, 2 * z + 1 - c) for z in range(chips) for c in range(2)]
    kept_mate = lax.ppermute(kept_mate, "ctx", across)
    leaving, *unit_one = call(
        middle_kernel, [PACKED, ((TOK, D), f32), ((TOK, LANE), f32)]
    )(
        tokens, *picks, over_exp(mixed)
    )
    double = ((SLOTS, 2 * HALF), bf16)
    slim = ((SLOTS, G), bf16)
    leaving, *second = call(second_kernel, [PACKED, DENSE, slim, DENSE, slim])(
        over_exp(leaving), upstream_one, wa, wb, column
    )
    one_own, one_mate = call(split_kernel, [double, double])(*second)
    one_mate = lax.ppermute(one_mate, "ctx", across)
    (leaving,) = call(return_kernel, [PACKED])(
        cotangent, *unit_one, *picks, over_exp(leaving)
    )
    grads_own, grads_mate = call(first_grad_kernel, [KEPT, KEPT], [DENSE])(
        over_exp(leaving), wb, positive, gate
    )
    half, narrow = ((4 * SLOTS, D // 2), bf16), ((4 * SLOTS, G), bf16)
    chunk = (2 * G, LANE)
    near, far, next_chip, own_chip = call(
        weight_kernel,
        [((4, *chunk), bf16), ((1, *chunk), bf16), ((2, *chunk), f32), ((1, *chunk), f32)],
        [half, narrow, half, narrow],
    )(grads_own, both_cores(grads_mate), kept_own, kept_mate, one_own, one_mate)
    near, far = lax.ppermute(near, "ctx", around), lax.ppermute(far, "ctx", two_on)
    cross, give = call(cross_kernel, [(chunk, bf16)] * 2)(near, next_chip)
    (same,) = call(same_kernel, [(chunk, bf16)])(near, far, next_chip)
    same = lax.ppermute(same, "ctx", two_on)
    cross = lax.ppermute(cross, "ctx", [(a, b + 1 - 2 * (b % 2)) for a, b in two_on])
    grad_in, grad_out = call(total_kernel, [((1, LANE, G), f32), ((1, G, LANE), f32)])(
        own_chip, near, both_cores(give), same, cross
    )
    return (grad_in, grad_out)


def solution(mesh):
    placed = (
        P(("ctx", "exp"), None),
        P(("ctx", "exp"), None),
        P(None, ("ctx", "exp"), None),
        P("exp", "ctx", None),
        P("exp", None, "ctx"),
        P("ctx", "exp"),
    )
    return jax.shard_map(
        on_device,
        mesh=mesh,
        in_specs=placed,
        out_specs=(P("exp", "ctx", None), P("exp", None, "ctx")),
        check_vma=False,
    )
```

```python
import functools

import jax
import jax.numpy as jnp
from jax import lax
from jax.experimental import pallas as pl
from jax.experimental.pallas import tpu as pltpu
from jax.sharding import PartitionSpec as P

epsilon = 1e-06
TOK, D, G, EXPERTS, CAP = 128, 2048, 256, 32, 3
SLOTS = EXPERTS * CAP
LANE = 128
CHUNKS = D // LANE
PEER = CAP * CHUNKS
CHIPS = 8
SHARD = 2 * G + 16
bf16, f32 = jnp.bfloat16, jnp.float32


def iota(shape, dimension):
    return lax.broadcasted_iota(jnp.int32, shape, dimension)


def choose(ids):
    hit = iota((EXPERTS, TOK), 0) == ids
    earlier = jnp.where(iota((TOK, TOK), 0) < iota((TOK, TOK), 1), 1.0, 0.0).astype(bf16)
    before = jnp.dot(jnp.where(hit, 1.0, 0.0).astype(bf16), earlier, preferred_element_type=f32)
    position = jnp.sum(jnp.where(hit, before, 0.0), axis=0, keepdims=True).astype(jnp.int32)
    slot = jnp.where(position < CAP, ids * CAP + position, -1)
    return jnp.where(iota((SLOTS, TOK), 0) == slot, 1.0, 0.0).astype(bf16)


def to_slots(pick, rows):
    return jnp.dot(pick, rows, preferred_element_type=f32)


def to_tokens(pick, rows):
    return lax.dot_general(pick, rows, (((0,), (0,)), ((), ())), preferred_element_type=f32)


def pack(rows):
    return rows.astype(bf16).reshape(SLOTS, CHUNKS, LANE).reshape(SLOTS * CHUNKS, LANE)


def unpack(blocks):
    return blocks.reshape(SLOTS, CHUNKS, LANE).reshape(SLOTS, D)


def normalize(state):
    inverse = 1.0 / jnp.sqrt(jnp.mean(state * state, axis=-1, keepdims=True) + epsilon)
    return state * inverse, inverse


def share_kernel(weight_in, weight_out, router, out):
    out[:LANE, :] = weight_in[0, :, :LANE]
    out[LANE:G, :] = weight_in[0, :, LANE:]
    out[G : 2 * G, :] = weight_out[0]
    out[2 * G :, :] = jnp.broadcast_to(router[...], (SHARD - 2 * G, LANE))


def place(block, first, chip, wa, wb, column):
    for core in range(2):
        at = first + core * SHARD
        to = pl.ds(pl.multiple_of((2 * chip + core) * LANE, LANE), LANE)
        wa[to, :LANE] = block[at : at + LANE, :]
        wa[to, LANE:] = block[at + LANE : at + G, :]
        wb[:, to] = block[at + G : at + 2 * G, :]
        column[:, to] = block[at + 2 * G : at + 2 * G + 1, :].astype(f32)


def own_chunks(core):
    chip = lax.div(lax.axis_index("ctx"), 2)
    way = 1 - 2 * core

    def chunk(hops, parity):
        return 2 * lax.rem(chip + hops * way + CHIPS, CHIPS) + parity

    pairs = [chunk(hops, parity) for hops in (1, 3, 2) for parity in range(2)]
    return pairs[:4] + [chunk(4, core)] + pairs[4:] + [chunk(0, core)]


def split(full, narrow, own, mate, first=0):
    core = lax.rem(lax.axis_index("ctx"), 2)
    for half, chunks in ((own, own_chunks(core)), (mate, own_chunks(1 - core))):
        for i, chunk in enumerate(chunks):
            at = pl.ds(pl.multiple_of(chunk * LANE, LANE), LANE)
            half[:, first + i * LANE : first + (i + 1) * LANE] = full[:, at]
        half[:, first + D // 2 : first + HALF] = narrow


def forward(rows, wa, wb, column):
    before = jnp.dot(rows, wa[...], preferred_element_type=f32)
    positive = jnp.maximum(before, 0.0)
    hidden = (positive * positive).astype(bf16)
    expert_out = jnp.dot(hidden, wb[...], preferred_element_type=f32)
    logit = jnp.sum(rows.astype(f32) * column[...], axis=1, keepdims=True)
    gate = 1.0 / (1.0 + jnp.exp(-logit))
    return positive, hidden, expert_out, gate


def backward(upstream, wb, positive, gate):
    upper = upstream.astype(f32)
    grad_expert = (gate * upper).astype(bf16)
    grad_hidden = lax.dot_general(
        grad_expert, wb[...], (((1,), (1,)), ((), ())), preferred_element_type=f32
    )
    grad_pre = (grad_hidden * 2.0 * positive).astype(bf16)
    return upper, grad_expert, grad_pre


def dispatch_kernel(tokens, cotangent, ids, out):
    unit, _ = normalize(tokens[...].astype(f32))
    rows = to_slots(choose(ids[0:1, :]), unit.astype(bf16))
    out[:, :PEER, :] = pack(rows).reshape(EXPERTS, PEER, LANE)
    rows = to_slots(choose(ids[1:2, :]), cotangent[...])
    out[:, PEER:, :] = pack(rows).reshape(EXPERTS, PEER, LANE)


def arrive_kernel(taken, rows, upstream):
    blocks = taken[...].reshape(EXPERTS, 2 * PEER, LANE)
    rows[...] = unpack(blocks[:, :PEER, :].reshape(EXPERTS * PEER, LANE))
    upstream[...] = unpack(blocks[:, PEER:, :].reshape(EXPERTS * PEER, LANE))


def first_kernel(
    rows, own, pair_1, pair_2, pair_3, far,
    out, positive_out, own_out, mate_out, gate_out, wa, wb, column
):
    chip = lax.div(lax.axis_index("ctx"), 2)
    place(own, 0, chip, wa, wb, column)
    for hop, pair in enumerate((pair_1, pair_2, pair_3), 1):
        place(pair, 0, lax.rem(chip + CHIPS - hop, CHIPS), wa, wb, column)
        place(pair, 2 * SHARD, lax.rem(chip + hop, CHIPS), wa, wb, column)
    place(far, 0, lax.rem(chip + CHIPS // 2, CHIPS), wa, wb, column)
    positive, hidden, expert_out, gate = forward(rows[...], wa, wb, column)
    out[...] = pack(gate * expert_out)
    positive_out[...] = positive
    split(rows, hidden, own_out, mate_out)
    gate_out[...] = jnp.broadcast_to(gate, (SLOTS, LANE))


def choose_kernel(ids, first, second):
    first[...] = choose(ids[0:1, :])
    second[...] = choose(ids[1:2, :])


def middle_kernel(tokens, pick_zero, pick_one, mixed, out, unit_out, inverse_out):
    state = tokens[...].astype(f32) + to_tokens(pick_zero[...], unpack(mixed[...]))
    unit, inverse = normalize(state)
    unit_out[...] = unit
    inverse_out[...] = jnp.broadcast_to(inverse, (TOK, LANE))
    out[...] = pack(to_slots(pick_one[...], unit.astype(bf16)))


def second_kernel(
    taken, upstream, wa, wb, column, out, rows, hidden_out, expert, pre
):
    rows[...] = unpack(taken[...])
    positive, hidden, expert_out, gate = forward(rows[...], wa, wb, column)
    upper, grad_expert, grad_pre = backward(upstream[...], wb, positive, gate)
    grad_gate = jnp.sum(upper * expert_out, axis=1, keepdims=True)
    grad_logit = grad_gate * gate * (1.0 - gate)
    flowing = lax.dot_general(
        grad_pre, wa[...], (((1,), (1,)), ((), ())), preferred_element_type=f32
    )
    out[...] = pack(flowing + grad_logit * column[...])
    hidden_out[...] = hidden
    expert[...] = grad_expert
    pre[...] = grad_pre


def split_kernel(rows, hidden, expert, pre, own, mate):
    split(rows, hidden[...], own, mate)
    split(expert, pre[...], own, mate, HALF)


def return_kernel(
    cotangent, unit_in, inverse, pick_zero, pick_one, taken, out
):
    unit = unit_in[...]
    grad = to_tokens(pick_one[...], unpack(taken[...]))
    inner = jnp.mean(grad * unit, axis=-1, keepdims=True)
    upstream = cotangent[...].astype(f32) + (grad - unit * inner) * inverse[:, :1]
    out[...] = pack(to_slots(pick_zero[...], upstream.astype(bf16)))


def over_rows(left, right):
    return lax.dot_general(left, right, (((0,), (0,)), ((), ())), preferred_element_type=f32)


def first_grad_kernel(taken, wb, positive, gate, own, mate, dense):
    _, grad_expert, grad_pre = backward(unpack(taken[...]), wb, positive[...], gate[:, :1])
    dense[...] = grad_expert
    split(dense, grad_pre, own, mate)


def products(operands, first, targets, rows, hidden, grads, pre):
    grads_own, grads_both, kept_own, kept_mate, one_own, one_mate = operands
    mate = pl.multiple_of((1 - lax.rem(lax.axis_index("ctx"), 2)) * SLOTS, SLOTS)
    kept = (kept_own[...], kept_mate[...], one_own[:, :HALF], one_mate[:, :HALF])
    grad = (grads_own[...], grads_both[pl.ds(mate, SLOTS), :], one_own[:, HALF:], one_mate[:, HALF:])
    columns = slice(first * LANE, (first + 4) * LANE)
    for i in range(4):
        to = slice(i * SLOTS, (i + 1) * SLOTS)
        rows[to, :], hidden[to, :] = kept[i][:, columns], kept[i][:, D // 2 :]
        grads[to, :], pre[to, :] = grad[i][:, columns], grad[i][:, D // 2 :]
    part_in = over_rows(pre[...], rows[...])
    part_out = over_rows(hidden[...], grads[...])
    for i, (out, to) in enumerate(targets):
        at = slice(i * LANE, (i + 1) * LANE)
        out[to, :G, :] = part_in[:, at].astype(out.dtype)
        out[to, G:, :] = part_out[:, at].astype(out.dtype)


def near_kernel(*refs):
    products(refs[:6], 0, [(refs[6], i) for i in range(4)], *refs[7:])


def rest_kernel(*refs):
    far, next_chip, own_chip = refs[6:9]
    products(refs[:6], 4, [(far, 0), (next_chip, 0), (next_chip, 1), (own_chip, 0)], *refs[9:])


def cross_kernel(near, next_chip, cross, give):
    core = lax.rem(lax.axis_index("ctx"), 2)
    cross[...] = (next_chip[1 - core] + near[3 - core].astype(f32)).astype(bf16)
    give[...] = near[1 - core]


def same_kernel(near, far, next_chip, same):
    core = lax.rem(lax.axis_index("ctx"), 2)
    same[...] = (
        next_chip[core] + near[2 + core].astype(f32) + far[0].astype(f32)
    ).astype(bf16)


def total_kernel(own_chip, near, gives, same, cross, grad_in, grad_out):
    core = lax.rem(lax.axis_index("ctx"), 2)
    mate = pl.multiple_of((1 - core) * 2 * G, 2 * G)
    total = own_chip[0] + near[core].astype(f32) + gives[pl.ds(mate, 2 * G), :].astype(f32)
    total = total + same[...].astype(f32) + cross[...].astype(f32)
    grad_in[0] = total[:G, :].T
    grad_out[0] = total[G:, :]


def call(kernel, outs, scratch=(), room=24, cost=0):
    return pl.pallas_call(
        kernel,
        out_shape=[jax.ShapeDtypeStruct(s, t) for s, t in outs],
        scratch_shapes=[pltpu.VMEM(s, t) for s, t in scratch],
        compiler_params=pltpu.CompilerParams(vmem_limit_bytes=room << 20),
        cost_estimate=pl.CostEstimate(flops=cost, bytes_accessed=0, transcendentals=0)
        if cost
        else None,
    )


PACKED = ((EXPERTS * PEER, LANE), bf16)
DENSE = ((SLOTS, D), bf16)
PICK = ((SLOTS, TOK), bf16)
HALF = D // 2 + G
KEPT = ((SLOTS, HALF), bf16)
WEIGHTS = (((D, G), bf16), ((G, D), bf16), ((1, D), f32))


def over_exp(buffer):
    shaped = buffer.reshape(EXPERTS, -1, LANE)
    return lax.all_to_all(shaped, "exp", 0, 0, tiled=True).reshape(buffer.shape)


def on_device(tokens, cotangent, expert_ids, weight_in, weight_out, router):
    chips = lax.axis_size("ctx") // 2
    ids = expert_ids[:, :, 0]
    cores = [[2 * z, 2 * z + 1] for z in range(chips)]

    def both_cores(value):
        return lax.all_gather(value, "ctx", axis=0, tiled=True, axis_index_groups=cores)

    around = [(2 * z, 2 * ((z + 1) % chips)) for z in range(chips)]
    around += [(2 * z + 1, 2 * ((z - 1) % chips) + 1) for z in range(chips)]
    (share,) = call(share_kernel, [((SHARD, LANE), bf16)], room=60)(
        weight_in, weight_out, router.reshape(1, LANE)
    )
    own = both_cores(share)
    (leaving,) = call(dispatch_kernel, [((EXPERTS, 2 * PEER, LANE), bf16)], room=60)(
        tokens, cotangent, ids
    )
    leaving = leaving.reshape(2 * EXPERTS * PEER, LANE)
    two_on = [
        (2 * z + c, 2 * ((z + 2 - 4 * c) % chips) + c) for z in range(chips) for c in range(2)
    ]
    two = lax.ppermute(own, "ctx", two_on)
    later, two = lax.optimization_barrier((own, two))
    _, two = lax.optimization_barrier((leaving, two))
    one = lax.ppermute(later, "ctx", around)
    three, four = lax.ppermute(two, "ctx", around), lax.ppermute(two, "ctx", two_on)
    pairs = [both_cores(one), both_cores(two)]
    ids, *pairs = lax.optimization_barrier((ids, *pairs))
    picks = call(choose_kernel, [PICK, PICK], cost=8 * 1150000000)(ids)
    three, *picks = lax.optimization_barrier((three, *picks))
    pairs += [both_cores(three), four]
    rows_zero, upstream_one = call(arrive_kernel, [DENSE, DENSE])(over_exp(leaving))
    mixed, positive, kept_own, kept_mate, gate, wa, wb, column = call(
        first_kernel,
        [PACKED, ((SLOTS, G), f32), KEPT, KEPT, ((SLOTS, LANE), f32), *WEIGHTS],
    )(rows_zero, own, *pairs)
    across = [(2 * z + c, 2 * z + 1 - c) for z in range(chips) for c in range(2)]
    kept_mate = lax.ppermute(kept_mate, "ctx", across)
    leaving, *unit_one = call(
        middle_kernel, [PACKED, ((TOK, D), f32), ((TOK, LANE), f32)]
    )(
        tokens, *picks, over_exp(mixed)
    )
    double = ((SLOTS, 2 * HALF), bf16)
    slim = ((SLOTS, G), bf16)
    leaving, *second = call(second_kernel, [PACKED, DENSE, slim, DENSE, slim])(
        over_exp(leaving), upstream_one, wa, wb, column
    )
    one_own, one_mate = call(split_kernel, [double, double])(*second)
    one_mate = lax.ppermute(one_mate, "ctx", across)
    (leaving,) = call(return_kernel, [PACKED])(
        cotangent, *unit_one, *picks, over_exp(leaving)
    )
    grads_own, grads_mate = call(first_grad_kernel, [KEPT, KEPT], [DENSE])(
        over_exp(leaving), wb, positive, gate
    )
    half, narrow = ((4 * SLOTS, D // 4), bf16), ((4 * SLOTS, G), bf16)
    chunk = (2 * G, LANE)
    operands = grads_own, both_cores(grads_mate), kept_own, kept_mate, one_own, one_mate
    buffers = [half, narrow, half, narrow]
    (near,) = call(near_kernel, [((4, *chunk), bf16)], buffers)(*operands)
    far, next_chip, own_chip = call(
        rest_kernel, [((1, *chunk), bf16), ((2, *chunk), f32), ((1, *chunk), f32)], buffers
    )(*operands)
    near, far = lax.ppermute(near, "ctx", around), lax.ppermute(far, "ctx", two_on)
    cross, give = call(cross_kernel, [(chunk, bf16)] * 2)(near, next_chip)
    (same,) = call(same_kernel, [(chunk, bf16)])(near, far, next_chip)
    same = lax.ppermute(same, "ctx", two_on)
    cross = lax.ppermute(cross, "ctx", [(a, b + 1 - 2 * (b % 2)) for a, b in two_on])
    grad_in, grad_out = call(total_kernel, [((1, LANE, G), f32), ((1, G, LANE), f32)])(
        own_chip, near, both_cores(give), same, cross
    )
    return (grad_in, grad_out)


def solution(mesh):
    placed = (
        P(("ctx", "exp"), None),
        P(("ctx", "exp"), None),
        P(None, ("ctx", "exp"), None),
        P("exp", "ctx", None),
        P("exp", None, "ctx"),
        P("ctx", "exp"),
    )
    return jax.shard_map(
        on_device,
        mesh=mesh,
        in_specs=placed,
        out_specs=(P("exp", "ctx", None), P("exp", None, "ctx")),
        check_vma=False,
    )
```
